32 devices in a mesh: var: 4 (over x, core), tm: 8 (over z, y).
Axes of the slice: x: 2, y: 2, z: 4, core: 2. Of those that a mesh axis runs over, the one named last changes fastest.
Arguments:
- latent: bfloat16 [4, 2048, 1536], P('var', 'tm')
- fresh_noise: bfloat16 [4, 2048, 1536], P('var', 'tm'), may hold values from -6 to 6
- timestep: int32 [1], replicated, may hold values from 400 to 800
- prompt_ids: int32 [4, 64], P('var'), may hold values from 0 to 16383
- block_table: int32 [3, 3], replicated, may hold values from 0 to 1, as said below
- prompt_table: bfloat16 [16384, 1536], P(None, 'tm'), may hold values from -12 to 12
- w_query: bfloat16 [1536, 768], P('var')
- w_keyval: bfloat16 [1536, 1536], P('var')
- w_out: bfloat16 [768, 1536], P('var'), may hold values from -0.4375 to 0.4375
Outputs:
- stepped: bfloat16 [4, 2048, 1536], P('var', 'tm')
The draws below stay inside these ranges and needn't reach their ends.
Inputs may be any that keep to these rules, and one draw needn't show every extreme that they name: `block_table`: the diagonal and the first column of the table are always 1.
All inputs are finite; a program needn't handle non-finite values.
Results may differ from the reference program's by a relative error of at most 0.0048.
Values may be sent and summed in bfloat16 or wider, within the bound.
No kernel may reach another device: no remote copies, remote signals or barrier semaphores. Data moves between devices by JAX's collectives and lax.ppermute only.
A program may use at most 64 MiB of HBM per device.

```python
import math
import jax
import jax.numpy as jnp
from jax import lax

D = 1536
HEADS = 12
HS = 64
HD = 768
VOCAB = 16384
PROMPT = 64
CH = 256
SEAM = 128
BLK = 128
NBLK = 3
TSTEPS = 1000
STRIDE = 200
VARS = 4
FRAMES = 2048
N_TM = 8


def draw_latent(key, part):
    base_key, row_key, column_key = jax.random.split(key, 3)
    base = jax.random.normal(base_key, (VARS, FRAMES, D), jnp.float32)
    row_scale = jnp.exp(jax.random.uniform(row_key, (VARS, FRAMES, 1), jnp.float32, math.log(0.3), math.log(3.0)))
    column_scale = jnp.exp(jax.random.uniform(column_key, (D,), jnp.float32, math.log(0.3), math.log(3.0)))
    return (base * row_scale * column_scale).astype(jnp.bfloat16)


def draw_block_table(key, part):
    picks = jax.random.randint(key, (NBLK, NBLK), 0, 2)
    positions = jnp.arange(NBLK)
    forced = (positions[:, None] == positions[None, :]) | (positions[None, :] == 0)
    return jnp.where(forced, 1, picks).astype(jnp.int32)


def projection_parts(key):
    query_part = jax.random.normal(jax.random.fold_in(key, 11), (D, HD), jnp.float32) / math.sqrt(D)
    key_part = jax.random.normal(jax.random.fold_in(key, 12), (D, HD), jnp.float32) / math.sqrt(D)
    value_part = jax.random.normal(jax.random.fold_in(key, 13), (D, HD), jnp.float32) / math.sqrt(D)
    return (query_part, key_part, value_part)


def draw_w_query(key, part):
    query_part, key_part, value_part = projection_parts(key)
    return query_part.astype(jnp.bfloat16)


def draw_w_keyval(key, part):
    query_part, key_part, value_part = projection_parts(key)
    return jnp.concatenate([key_part, value_part], axis=1).astype(jnp.bfloat16)


def with_ends(entries, stream_key, smallest, high):
    spot = [jax.random.randint(jax.random.fold_in(stream_key, axis), (), 0, length) for axis, length in enumerate(entries.shape)]
    longest = entries.shape.index(max(entries.shape))
    beside = spot[:longest] + [(spot[longest] + 1) % entries.shape[longest]] + spot[longest + 1:]
    return entries.at[tuple(spot)].set(smallest).at[tuple(beside)].set(high)


def level_of(own_key, dims, cuts, smallest, largest):
    loudness, own = 1.0, jax.random.fold_in(own_key, 6)
    for axis_at, parts in cuts:
        heights = jnp.exp(jax.random.uniform(jax.random.fold_in(own, axis_at), (parts,), jnp.float32, smallest / len(cuts), largest / len(cuts)))
        loudness = loudness * jnp.repeat(heights, dims[axis_at] // parts).reshape([-1 if axis == axis_at else 1 for axis in range(len(dims))])
    return loudness


def centred(stream_key, shape, scale, bound, cuts=(), kind=jnp.bfloat16):
    factor_of = level_of(stream_key, shape, cuts, -0.22, 0.18) if cuts else 1.0
    drawn = jax.random.normal(stream_key, shape, jnp.float32) * scale * factor_of
    return jnp.minimum(jnp.maximum(drawn, -bound), bound).astype(kind)


def setup_inputs(seed: int = 0) -> dict:
    arg_keys = jax.random.split(jax.random.key(seed), 10)
    latent = draw_latent(jax.random.fold_in(arg_keys[9], 71), 0)
    fresh_noise = centred(arg_keys[1], (VARS, FRAMES, D), 1.0, 6.0, ((0, 4), (1, 8)))
    timestep = jax.random.randint(arg_keys[2], (1,), 400, 801).astype(jnp.int32)
    prompt_ids = with_ends(jax.random.randint(arg_keys[3], (VARS, PROMPT), 0, VOCAB), jax.random.fold_in(arg_keys[3], 1), 0, VOCAB - 1).astype(jnp.int32)
    block_table = draw_block_table(jax.random.fold_in(arg_keys[9], 71), 0)
    prompt_table = centred(arg_keys[5], (VOCAB, D), 2.0, 12.0, ((1, 8),))
    w_query = draw_w_query(jax.random.fold_in(arg_keys[9], 71), 0)
    w_keyval = draw_w_keyval(jax.random.fold_in(arg_keys[9], 71), 0)
    w_out = centred(arg_keys[8], (HD, D), 0.07, 0.4375, ((0, 4),))
    return {"latent": latent, "fresh_noise": fresh_noise, "timestep": timestep, "prompt_ids": prompt_ids, "block_table": block_table, "prompt_table": prompt_table, "w_query": w_query, "w_keyval": w_keyval, "w_out": w_out}


epsilon = 1e-06

def plan(moment):
    return jnp.cos((moment / TSTEPS + 0.008) / 1.008 * (math.pi / 2.0)) ** 2

def coefficients(timestep):
    current = timestep[0].astype(jnp.float32)
    abar_now = plan(current)
    abar_prev = plan(current - STRIDE)
    spread = jnp.sqrt((1.0 - abar_prev) / (1.0 - abar_now) * (1.0 - abar_now / abar_prev))
    carried = jnp.sqrt((1.0 - abar_prev) * (abar_now / abar_prev - abar_now) / (1.0 - abar_now))
    coef_pred = carried - jnp.sqrt(abar_prev) * jnp.sqrt(1.0 - abar_now) / jnp.sqrt(abar_now)
    coef_latent = jnp.sqrt(abar_prev / abar_now)
    return (current, coef_latent, coef_pred, spread)

def time_embedding(current, model_width):
    half_width = model_width // 2
    frequency = jnp.exp(-math.log(10000.0) * jnp.arange(half_width, dtype=jnp.float32) / half_width)
    angles = current * frequency
    return jnp.concatenate([jnp.cos(angles), jnp.sin(angles)])

def reference(latent, fresh_noise, timestep, prompt_ids, block_table, prompt_table, w_query, w_keyval, w_out):
    current, coef_latent, coef_pred, spread = coefficients(timestep)
    embedded = time_embedding(current, D)
    pooled = lax.optimization_barrier(jnp.mean(prompt_table[prompt_ids].astype(jnp.float32), axis=1))
    condition = embedded[None, :] + pooled

    def normalize_project(operands):
        latent_rows, condition_row = operands
        values = latent_rows.astype(jnp.float32)
        inv_norm = lax.rsqrt(lax.optimization_barrier(jnp.mean(values * values, axis=-1, keepdims=True)) + epsilon)
        normed = (values * inv_norm * (1.0 + condition_row[None, :])).astype(jnp.bfloat16)
        queries = jnp.dot(normed, w_query, preferred_element_type=jnp.float32).astype(jnp.bfloat16)
        keyvals = jnp.dot(normed, w_keyval, preferred_element_type=jnp.float32).astype(jnp.bfloat16)
        return (queries, keyvals)
    queries, keyvals = lax.map(normalize_project, (latent, condition))
    queries = jnp.pad(queries, ((0, 0), (0, SEAM), (0, 0)))
    keyvals = jnp.pad(keyvals, ((0, 0), (0, SEAM), (0, 0)))
    window_rows = CH + SEAM
    allowed = jnp.repeat(jnp.repeat(block_table, BLK, axis=0), BLK, axis=1) > 0

    def one_window(flat_index):
        variant = flat_index // N_TM
        segment = flat_index % N_TM
        offset = (segment * CH).astype(jnp.int32)
        own_query = lax.dynamic_slice_in_dim(queries[variant], offset, window_rows, 0)
        own_keyval = lax.dynamic_slice_in_dim(keyvals[variant], offset, window_rows, 0)
        source_keyval = lax.dynamic_slice_in_dim(keyvals[0], offset, window_rows, 0)
        key_valid = offset + jnp.arange(window_rows, dtype=jnp.int32) < FRAMES
        key_mask = allowed & key_valid[None, :]
        both_masks = jnp.concatenate([key_mask, key_mask], axis=1)
        all_keys = jnp.concatenate([own_keyval[:, :HD], source_keyval[:, :HD]], axis=0)
        all_values = jnp.concatenate([own_keyval[:, HD:], source_keyval[:, HD:]], axis=0)
        query_heads = own_query.astype(jnp.float32).reshape(window_rows, HEADS, HS)
        key_heads = all_keys.astype(jnp.float32).reshape(2 * window_rows, HEADS, HS)
        value_heads = all_values.astype(jnp.float32).reshape(2 * window_rows, HEADS, HS)
        scores = jnp.einsum('qhd,khd->hqk', query_heads, key_heads) * (1.0 / math.sqrt(HS))
        scores = jnp.where(both_masks[None], scores, -1e+30)
        row_max = lax.optimization_barrier(jnp.max(scores, axis=-1, keepdims=True))
        weights = jnp.exp(scores - row_max)
        row_sum = lax.optimization_barrier(jnp.sum(weights, axis=-1, keepdims=True))
        probs = (weights / row_sum).astype(jnp.bfloat16)
        attended = jnp.einsum('hqk,khd->qhd', probs.astype(jnp.float32), value_heads)
        return attended.reshape(window_rows, HD)
    windows = lax.map(one_window, jnp.arange(VARS * N_TM, dtype=jnp.int32))
    windows = windows.reshape(VARS, N_TM, window_rows, HD)
    ramp_up = (jnp.arange(SEAM, dtype=jnp.float32) + 0.5) / SEAM
    tails = windows[:, :, CH:, :] * (1.0 - ramp_up)[None, None, :, None]
    carried = jnp.concatenate([jnp.zeros_like(tails[:, :1]), tails[:, :-1]], axis=1)
    lead_weight = jnp.where((jnp.arange(N_TM) == 0)[:, None], 1.0, ramp_up[None, :])
    lead_part = windows[:, :, :SEAM, :] * lead_weight[None, :, :, None] + carried
    blended = jnp.concatenate([lead_part, windows[:, :, SEAM:CH, :]], axis=2)
    blended = blended.astype(jnp.bfloat16).reshape(VARS, FRAMES, HD)

    def finish(operands):
        blended_rows, latent_rows, noise_rows = operands
        prediction = jnp.dot(blended_rows, w_out, preferred_element_type=jnp.float32)
        result = coef_latent * latent_rows.astype(jnp.float32) + coef_pred * prediction + spread * noise_rows.astype(jnp.float32)
        return result.astype(jnp.bfloat16)
    return lax.map(finish, (blended, latent, fresh_noise))
```

```python
import functools
import math

import jax
import jax.numpy as jnp
from jax import lax
from jax.experimental import pallas as pl
from jax.experimental.pallas import tpu as pltpu
from jax.sharding import PartitionSpec as P

HEADS = 12
HS = 64
SEAM = 128
BLK = 128
TSTEPS = 1000
STRIDE = 200
LANES = 128

epsilon = 1e-06
MASKED = -1e30
VMEM_LIMIT = 56 * 1024 * 1024

BF16 = jnp.bfloat16
F32 = jnp.float32


def plan(moment):
    return jnp.cos((moment / TSTEPS + 0.008) / 1.008 * (math.pi / 2.0)) ** 2


def coefficients(timestep):
    current = timestep[0].astype(jnp.float32)
    abar_now = plan(current)
    abar_prev = plan(current - STRIDE)
    spread = jnp.sqrt((1.0 - abar_prev) / (1.0 - abar_now) * (1.0 - abar_now / abar_prev))
    carried = jnp.sqrt((1.0 - abar_prev) * (abar_now / abar_prev - abar_now) / (1.0 - abar_now))
    coef_pred = carried - jnp.sqrt(abar_prev) * jnp.sqrt(1.0 - abar_now) / jnp.sqrt(abar_now)
    coef_latent = jnp.sqrt(abar_prev / abar_now)
    return (current, coef_latent, coef_pred, spread)


def time_embedding(current, model_width):
    half_width = model_width // 2
    frequency = jnp.exp(-math.log(10000.0) * jnp.arange(half_width, dtype=jnp.float32) / half_width)
    angles = current * frequency
    return jnp.concatenate([jnp.cos(angles), jnp.sin(angles)])


def swapped(block, axis, bit):
    route = [(i, i ^ bit) for i in range(lax.axis_size(axis))]
    return lax.ppermute(block, axis, route)


def shifted(block, axis, distance):
    devices = range(lax.axis_size(axis))
    route = [(i - distance, i) for i in devices if i - distance in devices]
    return lax.ppermute(block, axis, route)


def vmem():
    return pl.BlockSpec(memory_space=pltpu.VMEM)


def smem():
    return pl.BlockSpec(memory_space=pltpu.SMEM)


def anywhere():
    return pl.BlockSpec(memory_space=pl.ANY)


def params():
    return pltpu.CompilerParams(vmem_limit_bytes=VMEM_LIMIT)


def pool_kernel(count, ids_ref, table_ref, out_ref, blocks, sems):
    def copy(j):
        start = pl.multiple_of((ids_ref[0, j] >> 7) * LANES, LANES)
        return pltpu.make_async_copy(
            table_ref.at[:, pl.ds(start, LANES)], blocks.at[j], sems.at[j]
        )

    for j in range(count):
        copy(j).start()
    lane = lax.broadcasted_iota(jnp.int32, (1, LANES), 1)
    total = jnp.zeros(blocks.shape[1:], F32)
    for j in range(count):
        copy(j).wait()
        total += jnp.where(lane == (ids_ref[0, j] & (LANES - 1)), blocks[j].astype(F32), 0.0)
    ones = jnp.full((8, LANES), 1.0 / count, F32)
    out_ref[...] = lax.dot_general(
        ones,
        total,
        (((1,), (1,)), ((), ())),
        precision=lax.Precision.HIGHEST,
        preferred_element_type=F32,
    )


def pool(prompt_ids, table_columns):
    count = prompt_ids.shape[1]
    width = table_columns.shape[0]
    pooled = pl.pallas_call(
        functools.partial(pool_kernel, count),
        out_shape=jax.ShapeDtypeStruct((8, width), F32),
        in_specs=[smem(), anywhere()],
        out_specs=vmem(),
        scratch_shapes=[
            pltpu.VMEM((count, width, LANES), BF16),
            pltpu.SemaphoreType.DMA((count,)),
        ],
        compiler_params=params(),
        name="pool_prompt",
    )(prompt_ids, table_columns)
    return pooled[:1]


def gather_pooled(pooled):
    place = lax.axis_index("tm")
    bit = 1
    while bit < lax.axis_size("tm"):
        other = swapped(pooled, "tm", bit)
        upper = (place & bit) != 0
        pooled = jnp.concatenate(
            [jnp.where(upper, other, pooled), jnp.where(upper, pooled, other)], axis=0
        )
        bit *= 2
    return pooled.reshape(1, -1)


def gather_rows(weights):
    var_count = lax.axis_size("var")
    tm_count = lax.axis_size("tm")
    rows = weights[0].shape[0]
    quarter = rows // 4
    joined = lambda parts: parts[0] if len(parts) == 1 else jnp.concatenate(parts, axis=1)
    if var_count != 4 or tm_count % 4 or quarter % 16:
        return [(joined([lax.all_gather(w, "var", axis=0, tiled=True) for w in weights]), 0)]
    var_place = lax.axis_index("var")
    corner = lax.axis_index("tm") & 3

    def cut(which):
        return joined(
            [lax.dynamic_slice_in_dim(w, which * quarter, quarter, 0) for w in weights]
        )

    own = joined(weights)
    partner = swapped(own, "var", 1)
    first = swapped(cut(corner), "var", 2)
    fourth = swapped(cut(corner ^ 3), "var", 2)
    second = swapped(first, "tm", 1)
    third = swapped(first, "tm", 2)
    pieces = [(own, var_place * rows), (partner, (var_place ^ 1) * rows)]
    for k, piece in enumerate((first, second, third, fourth)):
        offset = (corner ^ k) * quarter
        pieces.append((piece, (var_place ^ 2) * rows + offset))
        pieces.append((swapped(piece, "var", 1), (var_place ^ 3) * rows + offset))
    return pieces


def project_kernel(
    n_pieces, column_from, places_ref, latent_ref, halo_ref, scale_ref, *refs
):
    pieces, (out_ref, weights, normed, sems) = refs[:n_pieces], refs[n_pieces:]
    copies = []
    for k, piece in enumerate(pieces):
        rows = piece.shape[0]
        start = pl.multiple_of(places_ref[k], 16)
        copies.append(
            pltpu.make_async_copy(
                piece.at[:, column_from:], weights.at[pl.ds(start, rows), :], sems.at[k]
            )
        )
    for copy in copies:
        copy.start()
    own_rows = latent_ref.shape[0]
    width = latent_ref.shape[1]
    scale = 1.0 + scale_ref[...]
    for begin, ref in ((0, latent_ref), (own_rows, halo_ref)):
        for row in range(0, ref.shape[0], 64):
            values = ref[row : row + 64, :].astype(F32)
            inv_norm = lax.rsqrt(jnp.sum(values * values, axis=-1, keepdims=True) / width + epsilon)
            normed[begin + row : begin + row + 64, :] = (values * inv_norm * scale).astype(BF16)
    for copy in copies:
        copy.wait()
    columns = out_ref.shape[1]
    step = 256

    def body(n, carry):
        at = pl.ds(pl.multiple_of(n * step, step), step)
        out_ref[:, at] = jnp.dot(
            normed[...], weights[:, at], preferred_element_type=F32
        ).astype(BF16)
        return carry

    lax.fori_loop(0, columns // step, body, 0)


def project(name, latent, halo, condition, pieces, column_from):
    rows = latent.shape[0] + halo.shape[0]
    width = latent.shape[1]
    columns = pieces[0][0].shape[1] - column_from
    places = jnp.stack([jnp.asarray(place, jnp.int32) for _, place in pieces])
    return pl.pallas_call(
        functools.partial(project_kernel, len(pieces), column_from),
        out_shape=jax.ShapeDtypeStruct((rows, columns), BF16),
        in_specs=[smem(), vmem(), vmem(), vmem()] + [anywhere()] * len(pieces),
        out_specs=vmem(),
        scratch_shapes=[
            pltpu.VMEM((width, columns), BF16),
            pltpu.VMEM((rows, width), BF16),
            pltpu.SemaphoreType.DMA((len(pieces),)),
        ],
        compiler_params=params(),
        cost_estimate=pl.CostEstimate(
            flops=2 * rows * width * columns, bytes_accessed=2 * width * columns, transcendentals=0
        ),
        name=name,
    )(places, latent, halo, condition, *[piece for piece, _ in pieces])


def attend_rows(query, own_ref, source_ref, bias, pair):
    head_width = own_ref.shape[1] // 2
    blocks = own_ref.shape[0] // BLK
    at = pl.ds(pair * LANES, LANES)
    value_at = pl.ds(head_width + pair * LANES, LANES)
    left = lax.broadcasted_iota(jnp.int32, (1, LANES), 1) < HS
    zero = jnp.zeros((), BF16)
    both = jnp.concatenate([jnp.where(left, query, zero), jnp.where(left, zero, query)], axis=0)
    score_parts = []
    for ref in (own_ref, source_ref):
        score_parts.append(
            lax.dot_general(
                both, ref[:, at], (((1,), (1,)), ((), ())), preferred_element_type=F32
            )
        )
    cut = lambda part, j: part[:, j * BLK : (j + 1) * BLK]
    peak = None
    for j in range(blocks):
        top = jnp.maximum(cut(score_parts[0], j), cut(score_parts[1], j))
        if j:
            top = top + bias[j]
        peak = top if peak is None else jnp.maximum(peak, top)
    peak = jnp.max(peak, axis=-1, keepdims=True)
    total = None
    ones = jnp.ones((own_ref.shape[0], LANES), BF16)
    for part, ref in zip(score_parts, (own_ref, source_ref)):
        weights = jnp.concatenate(
            [jnp.exp(cut(part, j) - (peak - bias[j])).astype(BF16) for j in range(blocks)], axis=1
        )
        values = jnp.concatenate([ref[:, value_at], ones], axis=1)
        term = jnp.dot(weights, values, preferred_element_type=F32)
        total = term if total is None else total + term
    mixed = total[:, :LANES] / total[:, LANES:]
    return jnp.where(left, mixed[:BLK], mixed[BLK:])


def tail_kernel(bias_ref, query_ref, own_ref, source_ref, out_ref):
    blocks = own_ref.shape[0] // BLK
    row = lax.broadcasted_iota(jnp.int32, (BLK, 1), 0).astype(F32)
    fade = 1.0 - (row + 0.5) / SEAM
    bias = [bias_ref[blocks - 1, j] for j in range(blocks)]
    for pair in range(HEADS // 2):
        at = pl.ds(pair * LANES, LANES)
        query = query_ref[(blocks - 1) * BLK :, at] * BF16(1.0 / math.sqrt(HS))
        out_ref[:, at] = (attend_rows(query, own_ref, source_ref, bias, pair) * fade).astype(BF16)


def main_kernel(bias_ref, query_ref, own_ref, source_ref, out_ref):
    blocks = own_ref.shape[0] // BLK
    for i in range(blocks - 1):
        bias = [bias_ref[i, j] for j in range(blocks)]
        for pair in range(HEADS // 2):
            at = pl.ds(pair * LANES, LANES)
            rows = pl.ds(i * BLK, BLK)
            query = query_ref[rows, at] * BF16(1.0 / math.sqrt(HS))
            out_ref[rows, at] = attend_rows(query, own_ref, source_ref, bias, pair)


def attend(name, kernel, rows, dtype, bias, query, own, source):
    width = own.shape[1] // 2
    return pl.pallas_call(
        kernel,
        out_shape=jax.ShapeDtypeStruct((rows, width), dtype),
        in_specs=[smem(), vmem(), vmem(), vmem()],
        out_specs=vmem(),
        compiler_params=params(),
        cost_estimate=pl.CostEstimate(
            flops=16 * rows * own.shape[0] * width, bytes_accessed=0, transcendentals=0
        ),
        name=name,
    )(bias, query, own, source)


def finish_kernel(
    n_pieces, places_ref, coef_ref, attended_ref, received_ref, latent_ref, noise_ref, *refs
):
    pieces, (out_ref, weights, sems) = refs[:n_pieces], refs[n_pieces:]
    copies = []
    for k, piece in enumerate(pieces):
        start = pl.multiple_of(places_ref[k], 16)
        copies.append(
            pltpu.make_async_copy(
                piece, weights.at[pl.ds(start, piece.shape[0]), :], sems.at[k]
            )
        )
    for copy in copies:
        copy.start()
    row = lax.broadcasted_iota(jnp.int32, (SEAM, 1), 0).astype(F32)
    ramp_up = jnp.where(coef_ref[3] > 0.5, 1.0, (row + 0.5) / SEAM)
    lead = attended_ref[:SEAM, :] * ramp_up + received_ref[...].astype(F32)
    blended = jnp.concatenate([lead, attended_ref[SEAM:, :]], axis=0).astype(BF16)
    for copy in copies:
        copy.wait()
    step = 256
    for begin in range(0, out_ref.shape[1], step):
        at = pl.ds(begin, step)
        prediction = jnp.dot(blended, weights[:, at], preferred_element_type=F32)
        result = (
            coef_ref[0] * latent_ref[:, at].astype(F32)
            + coef_ref[1] * prediction
            + coef_ref[2] * noise_ref[:, at].astype(F32)
        )
        out_ref[:, at] = result.astype(BF16)


def finish(coefs, attended, received, latent, noise, pieces):
    places = jnp.stack([jnp.asarray(place, jnp.int32) for _, place in pieces])
    return pl.pallas_call(
        functools.partial(finish_kernel, len(pieces)),
        out_shape=jax.ShapeDtypeStruct(latent.shape, BF16),
        in_specs=[smem(), smem()] + [vmem()] * 4 + [anywhere()] * len(pieces),
        out_specs=vmem(),
        scratch_shapes=[
            pltpu.VMEM((attended.shape[1], latent.shape[1]), BF16),
            pltpu.SemaphoreType.DMA((len(pieces),)),
        ],
        compiler_params=params(),
        name="blend_and_step",
    )(places, coefs, attended, received, latent, noise, *[piece for piece, _ in pieces])


def broadcast(value, axis):
    count = lax.axis_size(axis)
    place = lax.axis_index(axis)
    step = count // 2
    while step:
        route = [(i, i + step) for i in range(0, count, 2 * step)]
        arrived = lax.ppermute(value, axis, route)
        value = jnp.where((place & step) != 0, arrived, value)
        step //= 2
    return value


def local(
    latent, fresh_noise, timestep, prompt_ids, block_table, prompt_table, w_query, w_keyval, w_out
):
    latent = latent[0]
    own_rows, model_width = latent.shape
    head_width = w_query.shape[1]
    tm_count = lax.axis_size("tm")
    tm_place = lax.axis_index("tm")

    halo = shifted(latent[:SEAM], "tm", -1)
    pieces = gather_rows([w_query, w_keyval])
    pooled = gather_pooled(pool(prompt_ids, prompt_table.T))
    source_pooled = broadcast(pooled, "var")
    source_window = broadcast(jnp.concatenate([latent, halo], axis=0), "var")
    out_pieces = gather_rows([w_out])

    current, coef_latent, coef_pred, spread = coefficients(timestep)
    embedded = time_embedding(current, model_width)[None, :]
    first = (tm_place == 0).astype(F32)
    coefs = jnp.stack([coef_latent, coef_pred, spread, first])

    blocks = block_table.shape[0]
    present = (jnp.arange(blocks) < own_rows // BLK) | (tm_place != tm_count - 1)
    bias = jnp.where((block_table > 0) & present[None, :], 0.0, MASKED).astype(F32)

    window = project("project_own", latent, halo, embedded + pooled, pieces, 0)
    query, own = window[:, :head_width], window[:, head_width:]
    source = project(
        "project_source",
        source_window[:own_rows],
        source_window[own_rows:],
        embedded + source_pooled,
        pieces,
        head_width,
    )
    tail = attend("attend_tail", tail_kernel, SEAM, BF16, bias, query, own, source)
    received = shifted(tail, "tm", 1)
    attended = attend("attend_main", main_kernel, own_rows, F32, bias, query, own, source)
    return finish(coefs, attended, received, latent, fresh_noise[0], out_pieces)[None]


def solution(mesh):
    placed = (
        P("var", "tm", None),
        P("var", "tm", None),
        P(),
        P("var", None),
        P(),
        P(None, "tm"),
        P("var", None),
        P("var", None),
        P("var", None),
    )
    return jax.shard_map(
        local, mesh=mesh, in_specs=placed, out_specs=P("var", "tm", None), check_vma=False
    )
```

```python
import functools
import math

import jax
import jax.numpy as jnp
from jax import lax
from jax.experimental import pallas as pl
from jax.experimental.pallas import tpu as pltpu
from jax.sharding import PartitionSpec as P

HEADS = 12
HS = 64
SEAM = 128
BLK = 128
TSTEPS = 1000
STRIDE = 200
LANES = 128

epsilon = 1e-06
MASKED = -1e30
MICROSECOND = 10**9
VMEM_LIMIT = 18 * 1024 * 1024

BF16 = jnp.bfloat16
F32 = jnp.float32


def plan(moment):
    return jnp.cos((moment / TSTEPS + 0.008) / 1.008 * (math.pi / 2.0)) ** 2


def coefficients(timestep):
    current = timestep[0].astype(jnp.float32)
    abar_now = plan(current)
    abar_prev = plan(current - STRIDE)
    spread = jnp.sqrt((1.0 - abar_prev) / (1.0 - abar_now) * (1.0 - abar_now / abar_prev))
    carried = jnp.sqrt((1.0 - abar_prev) * (abar_now / abar_prev - abar_now) / (1.0 - abar_now))
    coef_pred = carried - jnp.sqrt(abar_prev) * jnp.sqrt(1.0 - abar_now) / jnp.sqrt(abar_now)
    coef_latent = jnp.sqrt(abar_prev / abar_now)
    return (current, coef_latent, coef_pred, spread)


def time_embedding(current, model_width):
    half_width = model_width // 2
    frequency = jnp.exp(-math.log(10000.0) * jnp.arange(half_width, dtype=jnp.float32) / half_width)
    angles = current * frequency
    return jnp.concatenate([jnp.cos(angles), jnp.sin(angles)])


def swapped(block, axis, bit):
    route = [(i, i ^ bit) for i in range(lax.axis_size(axis))]
    return lax.ppermute(block, axis, route)


def shifted(block, axis, distance):
    devices = range(lax.axis_size(axis))
    route = [(i - distance, i) for i in devices if i - distance in devices]
    return lax.ppermute(block, axis, route)


def vmem():
    return pl.BlockSpec(memory_space=pltpu.VMEM)


def smem():
    return pl.BlockSpec(memory_space=pltpu.SMEM)


def params():
    return pltpu.CompilerParams(vmem_limit_bytes=VMEM_LIMIT)


def anywhere():
    return pl.BlockSpec(memory_space=pl.ANY)


def hbm():
    return pl.BlockSpec(memory_space=pltpu.HBM)


def in_hbm(value):
    return pltpu.with_memory_space_constraint(value, pltpu.HBM)


def cost(flops):
    return pl.CostEstimate(flops=flops, bytes_accessed=1, transcendentals=0)


def everyones(row):
    var_count, tm_count = lax.axis_size("var"), lax.axis_size("tm")
    sent = jnp.broadcast_to(row, (var_count * tm_count, row.shape[1]))
    arrived = lax.all_to_all(sent, ("var", "tm"), 0, 0, tiled=True)
    return arrived.reshape(var_count, tm_count * row.shape[1])


def first_kernel(places_ref, ids_ref, table_ref, query_ref, keyval_ref, latent_ref, *refs):
    pooled_ref, halo_ref, *cut_refs, columns, sems = refs
    head_width = query_ref.shape[1]
    copies = [
        pltpu.make_async_copy(table_ref, columns, sems.at[0]),
        pltpu.make_async_copy(latent_ref.at[: halo_ref.shape[0], :], halo_ref, sems.at[1]),
    ]
    for k, target in enumerate(cut_refs):
        rows = target.shape[0]
        at = pl.ds(aligned(places_ref[k] * rows, 16), rows)
        copies += [
            pltpu.make_async_copy(
                query_ref.at[at, :], target.at[:, :head_width], sems.at[2 + 2 * k]
            ),
            pltpu.make_async_copy(
                keyval_ref.at[at, :], target.at[:, head_width:], sems.at[3 + 2 * k]
            ),
        ]
    for copy in copies:
        copy.start()
    lane = lax.broadcasted_iota(jnp.int32, (1, LANES), 1)
    copies[0].wait()

    def body(j, total):
        token = ids_ref[0, j]
        start = pl.multiple_of((token >> 7) * LANES, LANES)
        block = columns[:, pl.ds(start, LANES)].astype(F32)
        return total + jnp.where(lane == (token & (LANES - 1)), block, 0.0)

    count = ids_ref.shape[1]
    total = lax.fori_loop(0, count, body, jnp.zeros((columns.shape[0], LANES), F32), unroll=8)
    ones = jnp.full((8, LANES), 1.0 / count, F32)
    pooled_ref[...] = lax.dot_general(
        ones,
        total,
        (((1,), (1,)), ((), ())),
        precision=lax.Precision.HIGHEST,
        preferred_element_type=F32,
    )
    for copy in copies[1:]:
        copy.wait()


def first_rows(places, prompt_ids, prompt_table, w_query, w_keyval, latent):
    table_columns = prompt_table.T
    quarter = w_query.shape[0] // 4
    columns = w_query.shape[1] + w_keyval.shape[1]
    return pl.pallas_call(
        first_kernel,
        out_shape=[
            jax.ShapeDtypeStruct((8, table_columns.shape[0]), F32),
            jax.ShapeDtypeStruct((SEAM, latent.shape[1]), BF16),
        ]
        + [jax.ShapeDtypeStruct((quarter, columns), BF16)] * len(places),
        in_specs=[smem(), smem()] + [hbm()] * 4,
        out_specs=[vmem()] * (2 + len(places)),
        scratch_shapes=[
            pltpu.VMEM(table_columns.shape, BF16),
            pltpu.SemaphoreType.DMA((2 + 2 * len(places),)),
        ],
        compiler_params=params(),
        cost_estimate=cost(4 * MICROSECOND),
        name="pool_and_first_rows",
    )(
        numbers(*(places or (0,))),
        prompt_ids,
        *[in_hbm(value) for value in (table_columns, w_query, w_keyval, latent)],
    )


def joined(parts):
    return parts[0] if len(parts) == 1 else jnp.concatenate(parts, axis=1)


def can_route(rows):
    return lax.axis_size("var") == 4 and lax.axis_size("tm") % 4 == 0 and rows % 128 == 0


def cut(weights, which, count):
    rows = weights[0].shape[0] // count
    return joined([lax.dynamic_slice_in_dim(w, which * rows, rows, 0) for w in weights])


def gate_kernel(*refs):
    del refs


def together(*values):
    return pl.pallas_call(
        gate_kernel,
        out_shape=[jax.ShapeDtypeStruct(v.shape, v.dtype) for v in values],
        in_specs=[anywhere()] * len(values),
        out_specs=[anywhere()] * len(values),
        input_output_aliases={k: k for k in range(len(values))},
        compiler_params=params(),
        cost_estimate=cost(1),
        name="gate",
    )(*values)


def numbers(*values):
    return jnp.stack([jnp.asarray(value, jnp.int32) for value in values])


def aligned(value, multiple):
    return pl.multiple_of(value, multiple)


def normalize(target, begin, ref, scale, width):
    for row in range(0, ref.shape[0], 32):
        values = ref[row : row + 32, :].astype(F32)
        inv_norm = lax.rsqrt(jnp.sum(values * values, axis=-1, keepdims=True) / width + epsilon)
        target[begin + row : begin + row + 32, :] = (values * inv_norm * scale).astype(BF16)


def attend_rows(query, keyval_ref, bias, own_block, pair):
    head_width = keyval_ref.shape[1] // 2
    key_rows = keyval_ref.shape[0]
    blocks = len(bias)
    at = pl.ds(pair * LANES, LANES)
    value_at = pl.ds(head_width + pair * LANES, LANES)
    left = lax.broadcasted_iota(jnp.int32, (1, LANES), 1) < HS
    zero = jnp.zeros((), BF16)
    query = query * BF16(1.0 / math.sqrt(HS))
    both = jnp.concatenate([jnp.where(left, query, zero), jnp.where(left, zero, query)], axis=0)
    scores = lax.dot_general(
        both, keyval_ref[:, at], (((1,), (1,)), ((), ())), preferred_element_type=F32
    )
    cut_block = lambda j: scores[:, j * BLK : (j + 1) * BLK]
    peak = None
    for j in range(blocks):
        top = jnp.maximum(cut_block(j), cut_block(blocks + j))
        if j not in (0, own_block):
            top = top + bias[j]
        peak = top if peak is None else jnp.maximum(peak, top)
    peak = jnp.max(peak, axis=-1, keepdims=True)
    offsets = [peak if j in (0, own_block) else peak - bias[j] for j in range(blocks)]
    weights = jnp.concatenate(
        [jnp.exp(cut_block(j) - offsets[j % blocks]).astype(BF16) for j in range(2 * blocks)],
        axis=1,
    )
    ones = jnp.ones((key_rows, LANES), BF16)
    values = jnp.concatenate([keyval_ref[:, value_at], ones], axis=1)
    total = jnp.dot(weights, values, preferred_element_type=F32)
    mixed = total[:, :LANES] / total[:, LANES:]
    return jnp.where(left, mixed[:BLK], mixed[BLK:])


def own_kernel(n_wide, n_pairs, places_ref, latent_ref, halo_ref, scale_ref, *refs):
    wide_pieces = refs[:n_wide]
    query_pieces = refs[n_wide : n_wide + n_pairs]
    keyval_pieces = refs[n_wide + n_pairs : n_wide + 2 * n_pairs]
    query_ref, keyval_ref, weights_ref, normed, query_weights, sems = refs[n_wide + 2 * n_pairs :]
    head_width = query_weights.shape[1]
    copies = []

    def copy(source, target):
        copies.append(pltpu.make_async_copy(source, target, sems.at[len(copies)]))

    for k in range(n_pairs):
        at = pl.ds(aligned(places_ref[n_wide + k], 16), query_pieces[k].shape[0])
        copy(query_pieces[k], query_weights.at[at, :])
        copy(keyval_pieces[k], weights_ref.at[at, :])
    for k, piece in enumerate(wide_pieces):
        at = pl.ds(aligned(places_ref[k], 16), piece.shape[0])
        copy(piece.at[:, :head_width], query_weights.at[at, :])
        copy(piece.at[:, head_width:], weights_ref.at[at, :])
    for c in copies:
        c.start()
    scale = 1.0 + scale_ref[...]
    normalize(normed, 0, latent_ref, scale, latent_ref.shape[1])
    normalize(normed, latent_ref.shape[0], halo_ref, scale, latent_ref.shape[1])
    for c in copies:
        c.wait()
    step = 256
    for target, weights in ((query_ref, query_weights), (keyval_ref, weights_ref)):
        for begin in range(0, target.shape[1], step):
            at = pl.ds(begin, step)
            target[:, at] = jnp.dot(
                normed[...], weights[:, at], preferred_element_type=F32
            ).astype(BF16)


def project_own(latent, halo, condition, wide, wide_places, queries, keyvals, pair_places):
    window_rows = latent.shape[0] + halo.shape[0]
    width = latent.shape[1]
    keyval_width = keyvals[0].shape[1]
    head_width = keyval_width // 2
    n_copies = 2 * (len(wide) + len(queries))
    return pl.pallas_call(
        functools.partial(own_kernel, len(wide), len(queries)),
        out_shape=[
            jax.ShapeDtypeStruct((window_rows, head_width), BF16),
            jax.ShapeDtypeStruct((window_rows, keyval_width), BF16),
            jax.ShapeDtypeStruct((width, keyval_width), BF16),
        ],
        in_specs=[smem()] + [vmem()] * 3 + [hbm()] * n_copies_refs(wide, queries),
        out_specs=[vmem()] * 3,
        scratch_shapes=[
            pltpu.VMEM((window_rows, width), BF16),
            pltpu.VMEM((width, head_width), BF16),
            pltpu.SemaphoreType.DMA((n_copies,)),
        ],
        compiler_params=params(),
        cost_estimate=cost(6 * MICROSECOND),
        name="project_own",
    )(
        numbers(*wide_places, *pair_places),
        latent,
        halo,
        condition,
        *[in_hbm(piece) for piece in (*wide, *queries, *keyvals)],
    )


def n_copies_refs(wide, queries):
    return len(wide) + 2 * len(queries)


def source_kernel(
    n_sources, places_ref, bias_ref, query_ref, own_ref, weights_ref, scale_ref, *refs
):
    sources = refs[:n_sources]
    keyval_ref, tail_ref, normed = refs[n_sources:]
    window_rows, width = normed.shape
    main_rows = window_rows - SEAM
    scale = 1.0 + scale_ref[...]
    mine = jnp.where(places_ref[0] == 0, 1.0, 0.0)
    for row in range(0, window_rows, 32):
        at = pl.ds(row, 32)
        values = sources[0][at, :].astype(F32) * mine
        for ref in sources[1:]:
            values += ref[at, :].astype(F32)
        square = jnp.sum(values * values, axis=-1, keepdims=True)
        inv_norm = lax.rsqrt(square / width + epsilon)
        normed[at, :] = (values * inv_norm * scale).astype(BF16)
    keyval_ref[:window_rows, :] = own_ref[...]
    step = 256
    for begin in range(0, keyval_ref.shape[1], step):
        at = pl.ds(begin, step)
        keyval_ref[window_rows:, at] = jnp.dot(
            normed[...], weights_ref[:, at], preferred_element_type=F32
        ).astype(BF16)
    blocks = window_rows // BLK
    row = lax.broadcasted_iota(jnp.int32, (BLK, 1), 0).astype(F32)
    fade = 1.0 - (row + 0.5) / SEAM
    bias = [bias_ref[blocks - 1, j] for j in range(blocks)]
    for pair in range(HEADS // 2):
        at = pl.ds(pair * LANES, LANES)
        mixed = attend_rows(query_ref[main_rows:, at], keyval_ref, bias, blocks - 1, pair)
        tail_ref[:, at] = (mixed * fade).astype(BF16)


def project_source(place, bias, query, own, weights, scale, sources):
    window_rows, head_width = query.shape
    return pl.pallas_call(
        functools.partial(source_kernel, len(sources)),
        out_shape=[
            jax.ShapeDtypeStruct((2 * window_rows, 2 * head_width), BF16),
            jax.ShapeDtypeStruct((SEAM, head_width), BF16),
        ],
        in_specs=[smem(), smem()] + [vmem()] * (4 + len(sources)),
        out_specs=[vmem()] * 2,
        scratch_shapes=[pltpu.VMEM(sources[0].shape, BF16)],
        compiler_params=params(),
        cost_estimate=cost(5 * MICROSECOND),
        name="project_source_attend_tail",
    )(numbers(place), bias, query, own, weights, scale, *sources)


def main_kernel(bias_ref, query_ref, keyval_ref, out_ref):
    blocks = keyval_ref.shape[0] // (2 * BLK)
    for i in range(blocks - 1):
        bias = [bias_ref[i, j] for j in range(blocks)]
        rows = pl.ds(i * BLK, BLK)
        for pair in range(HEADS // 2):
            at = pl.ds(pair * LANES, LANES)
            out_ref[rows, at] = attend_rows(query_ref[rows, at], keyval_ref, bias, i, pair)


def attend_main(bias, query, keyval):
    rows, width = query.shape[0] - SEAM, query.shape[1]
    return pl.pallas_call(
        main_kernel,
        out_shape=jax.ShapeDtypeStruct((rows, width), F32),
        in_specs=[smem(), vmem(), vmem()],
        out_specs=vmem(),
        compiler_params=params(),
        cost_estimate=cost(4 * MICROSECOND),
        name="attend_main",
    )(bias, query, keyval)


def finish_kernel(
    n_pieces, places_ref, coef_ref, attended_ref, received_ref, latent_ref, noise_ref, *refs
):
    pieces, (out_ref, weights) = refs[:n_pieces], refs[n_pieces:]
    for k, piece in enumerate(pieces):
        weights[pl.ds(aligned(places_ref[k], 16), piece.shape[0]), :] = piece[...]
    row = lax.broadcasted_iota(jnp.int32, (SEAM, 1), 0).astype(F32)
    ramp_up = jnp.where(coef_ref[3] > 0.5, 1.0, (row + 0.5) / SEAM)
    lead = attended_ref[:SEAM, :] * ramp_up + received_ref[...].astype(F32)
    blended = jnp.concatenate([lead, attended_ref[SEAM:, :]], axis=0).astype(BF16)
    step = 256
    for begin in range(0, out_ref.shape[1], step):
        at = pl.ds(begin, step)
        prediction = jnp.dot(blended, weights[:, at], preferred_element_type=F32)
        result = (
            coef_ref[0] * latent_ref[:, at].astype(F32)
            + coef_ref[1] * prediction
            + coef_ref[2] * noise_ref[:, at].astype(F32)
        )
        out_ref[:, at] = result.astype(BF16)


def finish(coefs, attended, received, latent, noise, pieces, places):
    return pl.pallas_call(
        functools.partial(finish_kernel, len(pieces)),
        out_shape=jax.ShapeDtypeStruct(latent.shape, BF16),
        in_specs=[smem(), smem()] + [vmem()] * (4 + len(pieces)),
        out_specs=vmem(),
        scratch_shapes=[pltpu.VMEM((attended.shape[1], latent.shape[1]), BF16)],
        compiler_params=params(),
        cost_estimate=cost(3 * MICROSECOND),
        name="blend_and_step",
    )(
        numbers(*places),
        coefs,
        attended,
        received,
        latent,
        noise,
        *pieces,
    )


def from_source(value):
    bits = []
    bit = lax.axis_size("var") // 2
    while bit:
        bits.append(bit)
        bit //= 2
    return [(lax.ppermute(value, "var", [(0, bit)]), bit) for bit in bits]


def passed_on(arrivals):
    count = lax.axis_size("var")
    arrays = [arrivals[0][0]]
    for array, bit in arrivals[1:]:
        route = [(i, i + bit) for i in range(2 * bit, count, 2 * bit)]
        payload = functools.reduce(jnp.add, arrays)
        arrays += [array, lax.ppermute(payload, "var", route)]
    return arrays


def local(
    latent, fresh_noise, timestep, prompt_ids, block_table, prompt_table, w_query, w_keyval, w_out
):
    latent = latent[0]
    own_rows, model_width = latent.shape
    tm_count = lax.axis_size("tm")
    tm_place = lax.axis_index("tm")
    var_place = lax.axis_index("var")
    rows = w_query.shape[0]
    routed = can_route(rows)
    corner = tm_place & 3

    pooled, halo_rows, *cuts = first_rows(
        (corner, corner ^ 3) if routed else (),
        prompt_ids,
        prompt_table,
        w_query,
        w_keyval,
        latent,
    )
    if routed:
        quarter = rows // 4
        first = swapped(cuts[0], "var", 2)
        fourth = swapped(cuts[1], "var", 2)
        partner_query = swapped(w_query, "var", 1)
        partner_keyval = swapped(w_keyval, "var", 1)
    halo = shifted(halo_rows, "tm", -1)
    pooled = everyones(pooled[:1])
    if routed:
        halo, first = together(halo, first)
        second = swapped(first, "tm", 1)
        third = swapped(first, "tm", 2)
        first_over = swapped(first, "var", 1)
        fourth_over = swapped(fourth, "var", 1)
    window = jnp.concatenate([latent, halo], axis=0)
    sources = from_source(window)
    source_pooled = pooled[:1]
    pooled = lax.dynamic_slice_in_dim(pooled, var_place, 1, 0)
    current, coef_latent, coef_pred, spread = coefficients(timestep)
    embedded = time_embedding(current, model_width)[None, :]

    if routed:
        second, third = together(second, third)
        wide = [first, second, third, fourth]
        wide += [first_over, swapped(second, "var", 1), swapped(third, "var", 1), fourth_over]
        offsets = [(corner ^ k) * quarter for k in range(4)]
        wide_places = [(var_place ^ 2) * rows + offset for offset in offsets]
        wide_places += [(var_place ^ 3) * rows + offset for offset in offsets]
        queries, keyvals = [w_query, partner_query], [w_keyval, partner_keyval]
        pair_places = [var_place * rows, (var_place ^ 1) * rows]
        out_far = swapped(w_out, "var", 2)
    else:
        wide, wide_places, pair_places = [], [], [0]
        queries = [lax.all_gather(w_query, "var", axis=0, tiled=True)]
        keyvals = [lax.all_gather(w_keyval, "var", axis=0, tiled=True)]
    query, own, weights = project_own(
        latent, halo, embedded + pooled, wide, wide_places, queries, keyvals, pair_places
    )

    sources = [window] + passed_on(sources)
    blocks = block_table.shape[0]
    present = (jnp.arange(blocks) < own_rows // BLK) | (tm_place != tm_count - 1)
    bias = jnp.where((block_table > 0) & present[None, :], 0.0, MASKED).astype(F32)
    keyval, tail = project_source(
        var_place, bias, query, own, weights, embedded + source_pooled, sources
    )
    if routed:
        tail, out_far = together(tail, out_far)
        out_rows = w_out.shape[0]
        out_pieces = [w_out, swapped(w_out, "var", 1), out_far, swapped(out_far, "var", 1)]
        out_places = [(var_place ^ k) * out_rows for k in range(4)]
    else:
        out_pieces, out_places = [lax.all_gather(w_out, "var", axis=0, tiled=True)], [0]
    received = shifted(tail, "tm", 1)
    attended = attend_main(bias, query, keyval)
    coefs = jnp.stack([coef_latent, coef_pred, spread, (tm_place == 0).astype(F32)])
    return finish(coefs, attended, received, latent, fresh_noise[0], out_pieces, out_places)[None]


def solution(mesh):
    placed = (
        P("var", "tm", None),
        P("var", "tm", None),
        P(),
        P("var", None),
        P(),
        P(None, "tm"),
        P("var", None),
        P("var", None),
        P("var", None),
    )
    return jax.shard_map(
        local, mesh=mesh, in_specs=placed, out_specs=P("var", "tm", None), check_vma=False
    )
```

```python
import functools
import math

import jax
import jax.numpy as jnp
from jax import lax
from jax.experimental import pallas as pl
from jax.experimental.pallas import tpu as pltpu
from jax.sharding import PartitionSpec as P

HEADS = 12
HS = 64
SEAM = 128
BLK = 128
TSTEPS = 1000
STRIDE = 200
LANES = 128

epsilon = 1e-06
MASKED = -1e30
MICROSECOND = 10**9
VMEM_LIMIT = 18 * 1024 * 1024
ALL_VMEM = 62 * 1024 * 1024

BF16 = jnp.bfloat16
F32 = jnp.float32


def plan(moment):
    return jnp.cos((moment / TSTEPS + 0.008) / 1.008 * (math.pi / 2.0)) ** 2


def coefficients(timestep):
    current = timestep[0].astype(jnp.float32)
    abar_now = plan(current)
    abar_prev = plan(current - STRIDE)
    spread = jnp.sqrt((1.0 - abar_prev) / (1.0 - abar_now) * (1.0 - abar_now / abar_prev))
    carried = jnp.sqrt((1.0 - abar_prev) * (abar_now / abar_prev - abar_now) / (1.0 - abar_now))
    coef_pred = carried - jnp.sqrt(abar_prev) * jnp.sqrt(1.0 - abar_now) / jnp.sqrt(abar_now)
    coef_latent = jnp.sqrt(abar_prev / abar_now)
    return (current, coef_latent, coef_pred, spread)


def time_waves(current, model_width):
    half_width = model_width // 2
    frequency = jnp.exp(-math.log(10000.0) * jnp.arange(half_width, dtype=jnp.float32) / half_width)
    angles = current * frequency
    return (jnp.cos(angles)[None, :], jnp.sin(angles)[None, :])


def swapped(block, axis, bit):
    route = [(i, i ^ bit) for i in range(lax.axis_size(axis))]
    return lax.ppermute(block, axis, route)


def shifted(block, axis, distance):
    devices = range(lax.axis_size(axis))
    route = [(i - distance, i) for i in devices if i - distance in devices]
    return lax.ppermute(block, axis, route)


def vmem():
    return pl.BlockSpec(memory_space=pltpu.VMEM)


def smem():
    return pl.BlockSpec(memory_space=pltpu.SMEM)


def params(limit=VMEM_LIMIT):
    return pltpu.CompilerParams(vmem_limit_bytes=limit)


def anywhere():
    return pl.BlockSpec(memory_space=pl.ANY)


def hbm():
    return pl.BlockSpec(memory_space=pltpu.HBM)


def in_hbm(value):
    return pltpu.with_memory_space_constraint(value, pltpu.HBM)


def cost(flops):
    return pl.CostEstimate(flops=flops, bytes_accessed=1, transcendentals=0)


def whole_rows(row):
    tm_count = lax.axis_size("tm")
    sent = jnp.broadcast_to(row, (tm_count, row.shape[1]))
    arrived = lax.all_to_all(sent, "tm", 0, 0, tiled=True)
    if row.shape[1] % HS or tm_count % 8:
        arrived = arrived.reshape(1, tm_count * row.shape[1])
    return arrived


def first_kernel(
    places_ref, ids_ref, table_ref, query_ref, keyval_ref, out_weights_ref, latent_ref, *refs
):
    pooled_ref, halo_ref, out_cut_ref, *cut_refs, columns, sems = refs
    head_width = query_ref.shape[1]
    copies = [
        pltpu.make_async_copy(table_ref, columns, sems.at[0]),
        pltpu.make_async_copy(latent_ref.at[: halo_ref.shape[0], :], halo_ref, sems.at[1]),
    ]
    out_rows = out_cut_ref.shape[0]
    at = pl.ds(aligned(places_ref[0] * out_rows, 16), out_rows)
    copies.append(pltpu.make_async_copy(out_weights_ref.at[at, :], out_cut_ref, sems.at[2]))
    for k, target in enumerate(cut_refs):
        rows = target.shape[0]
        at = pl.ds(aligned(places_ref[1 + k] * rows, 16), rows)
        copies += [
            pltpu.make_async_copy(
                query_ref.at[at, :], target.at[:, :head_width], sems.at[3 + 2 * k]
            ),
            pltpu.make_async_copy(
                keyval_ref.at[at, :], target.at[:, head_width:], sems.at[4 + 2 * k]
            ),
        ]
    for copy in copies:
        copy.start()
    lane = lax.broadcasted_iota(jnp.int32, (1, LANES), 1)
    copies[0].wait()

    def body(j, total):
        token = ids_ref[0, j]
        start = pl.multiple_of((token >> 7) * LANES, LANES)
        block = columns[:, pl.ds(start, LANES)].astype(F32)
        return total + jnp.where(lane == (token & (LANES - 1)), block, 0.0)

    count = ids_ref.shape[1]
    total = lax.fori_loop(0, count, body, jnp.zeros((columns.shape[0], LANES), F32), unroll=8)
    ones = jnp.full((8, LANES), 1.0 / count, F32)
    pooled_ref[...] = lax.dot_general(
        ones,
        total,
        (((1,), (1,)), ((), ())),
        precision=lax.Precision.HIGHEST,
        preferred_element_type=F32,
    )
    for copy in copies[1:]:
        copy.wait()


def first_rows(side, places, prompt_ids, prompt_table, w_query, w_keyval, w_out, latent):
    table_columns = prompt_table.T
    quarter = w_query.shape[0] // 4
    columns = w_query.shape[1] + w_keyval.shape[1]
    return pl.pallas_call(
        first_kernel,
        out_shape=[
            jax.ShapeDtypeStruct((8, table_columns.shape[0]), F32),
            jax.ShapeDtypeStruct((SEAM, latent.shape[1]), BF16),
            jax.ShapeDtypeStruct((w_out.shape[0] // 2, w_out.shape[1]), BF16),
        ]
        + [jax.ShapeDtypeStruct((quarter, columns), BF16)] * len(places),
        in_specs=[smem(), smem()] + [hbm()] * 5,
        out_specs=[vmem()] * (3 + len(places)),
        scratch_shapes=[
            pltpu.VMEM(table_columns.shape, BF16),
            pltpu.SemaphoreType.DMA((3 + 2 * len(places),)),
        ],
        compiler_params=params(),
        cost_estimate=cost(4 * MICROSECOND),
        name="pool_and_first_rows",
    )(
        numbers(side, *places),
        prompt_ids,
        *[in_hbm(value) for value in (table_columns, w_query, w_keyval, w_out, latent)],
    )


def joined(parts):
    return parts[0] if len(parts) == 1 else jnp.concatenate(parts, axis=1)


def can_route(rows):
    return lax.axis_size("var") == 4 and lax.axis_size("tm") % 4 == 0 and rows % 128 == 0


def cut(weights, which, count):
    rows = weights[0].shape[0] // count
    return joined([lax.dynamic_slice_in_dim(w, which * rows, rows, 0) for w in weights])


def gate_kernel(*refs):
    del refs


def together(*values, limit=VMEM_LIMIT):
    return pl.pallas_call(
        gate_kernel,
        out_shape=[jax.ShapeDtypeStruct(v.shape, v.dtype) for v in values],
        in_specs=[anywhere()] * len(values),
        out_specs=[anywhere()] * len(values),
        input_output_aliases={k: k for k in range(len(values))},
        compiler_params=params(limit),
        cost_estimate=cost(1),
        name="gate",
    )(*values)


def numbers(*values):
    return jnp.stack([jnp.asarray(value, jnp.int32) for value in values])


def aligned(value, multiple):
    return pl.multiple_of(value, multiple)


def scale_of(rows_ref, cos_ref, sin_ref):
    rows = rows_ref[...]
    row = jnp.concatenate([rows[k : k + 1, :] for k in range(rows.shape[0])], axis=1)
    return 1.0 + (jnp.concatenate([cos_ref[...], sin_ref[...]], axis=1) + row)


def bias_of(table_ref, last, query_block):
    blocks = table_ref.shape[0]
    biases = []
    for j in range(blocks):
        allowed = table_ref[query_block, j] > 0
        if j == blocks - 1:
            allowed = jnp.logical_and(allowed, last == 0)
        biases.append(jnp.where(allowed, 0.0, MASKED))
    return biases


def normalize(target, begin, ref, scale, width):
    for row in range(0, ref.shape[0], 32):
        values = ref[row : row + 32, :].astype(F32)
        inv_norm = lax.rsqrt(jnp.sum(values * values, axis=-1, keepdims=True) / width + epsilon)
        target[begin + row : begin + row + 32, :] = (values * inv_norm * scale).astype(BF16)


def normalize_kernel(
    latent_ref, halo_ref, rows_ref, cos_ref, sin_ref, normed_ref, window, normed, rows, sems
):
    main_rows = latent_ref.shape[0]
    copies = [
        pltpu.make_async_copy(latent_ref, window.at[:main_rows, :], sems.at[0]),
        pltpu.make_async_copy(halo_ref, window.at[main_rows:, :], sems.at[1]),
        pltpu.make_async_copy(rows_ref, rows, sems.at[2]),
    ]
    for copy in copies:
        copy.start()
    for copy in copies:
        copy.wait()
    normalize(normed, 0, window, scale_of(rows, cos_ref, sin_ref), window.shape[1])
    copy = pltpu.make_async_copy(normed, normed_ref, sems.at[3])
    copy.start()
    copy.wait()


def normalized(latent, halo, rows, waves):
    shape = (latent.shape[0] + SEAM, latent.shape[1])
    return pl.pallas_call(
        normalize_kernel,
        out_shape=pltpu.HBM(shape, BF16),
        in_specs=[anywhere()] * 3 + [vmem()] * 2,
        out_specs=hbm(),
        scratch_shapes=[
            pltpu.VMEM(shape, BF16),
            pltpu.VMEM(shape, BF16),
            pltpu.VMEM(rows.shape, F32),
            pltpu.SemaphoreType.DMA((4,)),
        ],
        compiler_params=params(),
        cost_estimate=cost(MICROSECOND),
        name="normalize",
    )(latent, halo, rows, *waves)


def attend_rows(query, keyval_ref, bias, own_block, pair):
    head_width = keyval_ref.shape[1] // 2
    key_rows = keyval_ref.shape[0]
    blocks = len(bias)
    at = pl.ds(pair * LANES, LANES)
    value_at = pl.ds(head_width + pair * LANES, LANES)
    left = lax.broadcasted_iota(jnp.int32, (1, LANES), 1) < HS
    zero = jnp.zeros((), BF16)
    query = query * BF16(1.0 / math.sqrt(HS))
    both = jnp.concatenate([jnp.where(left, query, zero), jnp.where(left, zero, query)], axis=0)
    scores = lax.dot_general(
        both, keyval_ref[:, at], (((1,), (1,)), ((), ())), preferred_element_type=F32
    )
    cut_block = lambda j: scores[:, j * BLK : (j + 1) * BLK]
    peak = None
    for j in range(blocks):
        top = jnp.maximum(cut_block(j), cut_block(blocks + j))
        if j not in (0, own_block):
            top = top + bias[j]
        peak = top if peak is None else jnp.maximum(peak, top)
    peak = jnp.max(peak, axis=-1, keepdims=True)
    offsets = [peak if j in (0, own_block) else peak - bias[j] for j in range(blocks)]
    weights = jnp.concatenate(
        [jnp.exp(cut_block(j) - offsets[j % blocks]).astype(BF16) for j in range(2 * blocks)],
        axis=1,
    )
    ones = jnp.ones((key_rows, LANES), BF16)
    values = jnp.concatenate([keyval_ref[:, value_at], ones], axis=1)
    total = jnp.dot(weights, values, preferred_element_type=F32)
    mixed = total[:, :LANES] / total[:, LANES:]
    return jnp.where(left, mixed[:BLK], mixed[BLK:])


def project_kernel(n_wide, n_pairs, n_sources, places_ref, table_ref, normed_hbm, *refs):
    wide_pieces, refs = refs[:n_wide], refs[n_wide:]
    query_pieces, refs = refs[:n_pairs], refs[n_pairs:]
    keyval_pieces, refs = refs[:n_pairs], refs[n_pairs:]
    sources, refs = refs[:n_sources], refs[n_sources:]
    query_ref, keyval_ref, tail_ref, query_weights, keyval_weights, normed, tail_query, sems = refs
    head_width = query_weights.shape[1]
    window_rows = normed.shape[0] // 2
    main_rows = window_rows - SEAM
    own_rows = pl.ds(0, window_rows)
    source_rows = pl.ds(window_rows, window_rows)
    choice, last = places_ref[0], places_ref[1]

    rows_of = [(places_ref[2 + n_wide + k], p.shape[0]) for k, p in enumerate(query_pieces)]
    rows_of += [(places_ref[2 + k], p.shape[0]) for k, p in enumerate(wide_pieces)]
    rows_of = [pl.ds(aligned(start, 16), count) for start, count in rows_of]
    query_parts = list(query_pieces) + [p.at[:, :head_width] for p in wide_pieces]
    keyval_parts = list(keyval_pieces) + [p.at[:, head_width:] for p in wide_pieces]
    copies = [(normed_hbm, normed.at[own_rows, :])]
    copies += [(p, query_weights.at[at, :]) for p, at in zip(query_parts, rows_of)]
    copies += [(p, keyval_weights.at[at, :]) for p, at in zip(keyval_parts, rows_of)]
    copies = [
        pltpu.make_async_copy(source, target, sems.at[k])
        for k, (source, target) in enumerate(copies)
    ]
    for copy in copies:
        copy.start()
    source_copies = [
        pltpu.make_async_copy(source, normed.at[source_rows, :], sems.at[len(copies)])
        for source in sources
    ]
    for k, copy in enumerate(source_copies):
        pl.when(choice == k)(copy.start)
    for copy in copies[: 1 + len(rows_of)]:
        copy.wait()
    step = 256
    for begin in range(0, head_width, step):
        at = pl.ds(begin, step)
        result = jnp.dot(
            normed[own_rows, :], query_weights[:, at], preferred_element_type=F32
        ).astype(BF16)
        query_ref[:, at] = result[:main_rows]
        tail_query[:, at] = result[main_rows:]
    for k, copy in enumerate(source_copies):
        pl.when(choice == k)(copy.wait)
    for copy in copies[1 + len(rows_of) :]:
        copy.wait()
    for begin in range(0, 2 * head_width, step):
        at = pl.ds(begin, step)
        keyval_ref[:, at] = jnp.dot(
            normed[...], keyval_weights[:, at], preferred_element_type=F32
        ).astype(BF16)
    blocks = window_rows // BLK
    row = lax.broadcasted_iota(jnp.int32, (BLK, 1), 0).astype(F32)
    fade = 1.0 - (row + 0.5) / SEAM
    bias = bias_of(table_ref, last, blocks - 1)
    for pair in range(HEADS // 2):
        at = pl.ds(pair * LANES, LANES)
        mixed = attend_rows(tail_query[:, at], keyval_ref, bias, blocks - 1, pair)
        tail_ref[:, at] = (mixed * fade).astype(BF16)


def project(
    choice, last, block_table, normed, wide, wide_places, queries, keyvals, pair_places, sources
):
    window_rows, width = normed.shape
    keyval_width = keyvals[0].shape[1]
    head_width = keyval_width // 2
    n_copies = 1 + 2 * (len(wide) + len(queries))
    arrays = (normed, *wide, *queries, *keyvals, *sources)
    late = (*wide[6:], sources[-1])
    specs = [anywhere() if any(a is b for b in late) else hbm() for a in arrays]
    arrays = [a if any(a is b for b in late) else in_hbm(a) for a in arrays]
    return pl.pallas_call(
        functools.partial(project_kernel, len(wide), len(queries), len(sources)),
        out_shape=[
            jax.ShapeDtypeStruct((window_rows - SEAM, head_width), BF16),
            jax.ShapeDtypeStruct((2 * window_rows, keyval_width), BF16),
            jax.ShapeDtypeStruct((SEAM, head_width), BF16),
        ],
        in_specs=[smem(), smem()] + specs,
        out_specs=[vmem()] * 3,
        scratch_shapes=[
            pltpu.VMEM((width, head_width), BF16),
            pltpu.VMEM((width, keyval_width), BF16),
            pltpu.VMEM((2 * window_rows, width), BF16),
            pltpu.VMEM((SEAM, head_width), BF16),
            pltpu.SemaphoreType.DMA((n_copies + 1,)),
        ],
        compiler_params=params(),
        cost_estimate=cost(10 * MICROSECOND),
        name="project_attend_tail",
    )(
        numbers(choice, last, *wide_places, *pair_places),
        block_table,
        *arrays,
    )


def main_kernel(places_ref, table_ref, query_ref, keyval_ref, out_ref):
    blocks = keyval_ref.shape[0] // (2 * BLK)
    for i in range(blocks - 1):
        bias = bias_of(table_ref, places_ref[0], i)
        rows = pl.ds(i * BLK, BLK)
        for pair in range(HEADS // 2):
            at = pl.ds(pair * LANES, LANES)
            out_ref[rows, at] = attend_rows(query_ref[rows, at], keyval_ref, bias, i, pair)


def attend_main(last, block_table, query, keyval):
    rows, width = query.shape
    return pl.pallas_call(
        main_kernel,
        out_shape=jax.ShapeDtypeStruct((rows, width), F32),
        in_specs=[smem(), smem(), vmem(), vmem()],
        out_specs=vmem(),
        compiler_params=params(),
        cost_estimate=cost(4 * MICROSECOND),
        name="attend_main",
    )(numbers(last), block_table, query, keyval)


def finish_kernel(
    n_pieces, places_ref, coef_ref, attended_ref, received_ref, latent_ref, noise_ref, *refs
):
    pieces, (out_ref, weights) = refs[:n_pieces], refs[n_pieces:]
    for k, piece in enumerate(pieces):
        weights[pl.ds(aligned(places_ref[k], 16), piece.shape[0]), :] = piece[...]
    row = lax.broadcasted_iota(jnp.int32, (SEAM, 1), 0).astype(F32)
    ramp_up = jnp.where(coef_ref[3] > 0.5, 1.0, (row + 0.5) / SEAM)
    lead = attended_ref[:SEAM, :] * ramp_up + received_ref[...].astype(F32)
    blended = jnp.concatenate([lead, attended_ref[SEAM:, :]], axis=0).astype(BF16)
    step = 256
    for begin in range(0, out_ref.shape[1], step):
        at = pl.ds(begin, step)
        prediction = jnp.dot(blended, weights[:, at], preferred_element_type=F32)
        result = (
            coef_ref[0] * latent_ref[:, at].astype(F32)
            + coef_ref[1] * prediction
            + coef_ref[2] * noise_ref[:, at].astype(F32)
        )
        out_ref[:, at] = result.astype(BF16)


def finish(coefs, attended, received, latent, noise, pieces, places):
    return pl.pallas_call(
        functools.partial(finish_kernel, len(pieces)),
        out_shape=jax.ShapeDtypeStruct(latent.shape, BF16),
        in_specs=[smem(), smem()] + [vmem()] * (4 + len(pieces)),
        out_specs=vmem(),
        scratch_shapes=[pltpu.VMEM((attended.shape[1], latent.shape[1]), BF16)],
        compiler_params=params(),
        cost_estimate=cost(3 * MICROSECOND),
        name="blend_and_step",
    )(
        numbers(*places),
        coefs,
        attended,
        received,
        latent,
        noise,
        *pieces,
    )


def from_source(value):
    bits = []
    bit = lax.axis_size("var") // 2
    while bit:
        bits.append(bit)
        bit //= 2
    return [(lax.ppermute(value, "var", [(0, bit)]), bit) for bit in bits]


def passed_on(value, arrivals):
    count = lax.axis_size("var")
    place = lax.axis_index("var")
    arrays, choice = [value, arrivals[0][0]], (place == arrivals[0][1]).astype(jnp.int32)
    for array, bit in arrivals[1:]:
        payload = functools.reduce(jnp.add, arrays[1:])
        route = [(i, i + bit) for i in range(2 * bit, count, 2 * bit)]
        choice = jnp.where(place == bit, len(arrays), choice)
        arrays.append(array)
        choice = jnp.where((place > bit) & (place % (2 * bit) == bit), len(arrays), choice)
        arrays.append(lax.ppermute(payload, "var", route))
    return arrays, choice


def local(
    latent, fresh_noise, timestep, prompt_ids, block_table, prompt_table, w_query, w_keyval, w_out
):
    latent = latent[0]
    own_rows, model_width = latent.shape
    tm_count = lax.axis_size("tm")
    tm_place = lax.axis_index("tm")
    var_place = lax.axis_index("var")
    rows = w_query.shape[0]
    routed = can_route(rows)
    corner = tm_place & 3

    side = tm_place & 1
    pooled, halo_rows, out_cut, *cuts = first_rows(
        side if routed else 0,
        (corner, corner ^ 3) if routed else (),
        prompt_ids,
        prompt_table,
        w_query,
        w_keyval,
        w_out,
        latent,
    )
    halo = shifted(halo_rows, "tm", -1)
    pooled = whole_rows(pooled[:1])
    if routed:
        quarter = rows // 4
        first = swapped(cuts[0], "var", 2)
        fourth = swapped(cuts[1], "var", 2)
        halo, pooled, first, fourth = together(
            halo, pooled, first, fourth, limit=ALL_VMEM
        )

    current, coef_latent, coef_pred, spread = coefficients(timestep)
    normed = normalized(latent, halo, pooled, time_waves(current, model_width))
    sources = from_source(normed)
    if routed:
        second = swapped(first, "tm", 1)
        third = swapped(first, "tm", 2)
        queries, keyvals = [w_query], [w_keyval]
        fetched = [second, third]
        fetched += [swapped(piece, "var", 1) for piece in (first, fourth, w_query, w_keyval)]
        fetched += [swapped(out_cut, "var", 2)] + [array for array, _ in sources]
        second, third, first_over, fourth_over, partner_query, partner_keyval, *fetched = together(
            *fetched, limit=ALL_VMEM
        )
        out_first, *fetched = fetched
        sources = [(array, bit) for array, (_, bit) in zip(fetched, sources)]

        wide = [first, second, third, fourth, first_over, fourth_over]
        wide += [swapped(second, "var", 1), swapped(third, "var", 1)]
        here, there = (var_place ^ 2) * rows, (var_place ^ 3) * rows
        wide_places = [here + (corner ^ k) * quarter for k in range(4)]
        wide_places += [there + (corner ^ k) * quarter for k in (0, 3, 1, 2)]
        queries, keyvals = [w_query, partner_query], [w_keyval, partner_keyval]
        pair_places = [var_place * rows, (var_place ^ 1) * rows]
    else:
        wide, wide_places, pair_places = [], [], [0]
        queries = [lax.all_gather(w_query, "var", axis=0, tiled=True)]
        keyvals = [lax.all_gather(w_keyval, "var", axis=0, tiled=True)]
    sources, choice = passed_on(normed, sources)
    last = tm_place == tm_count - 1
    query, keyval, tail = project(
        choice,
        last,
        block_table,
        normed,
        wide,
        wide_places,
        queries,
        keyvals,
        pair_places,
        sources,
    )
    if routed:
        tail, out_second = together(tail, swapped(out_first, "tm", 1))
        out_rows = w_out.shape[0]
        half = out_rows // 2
        out_pieces = [w_out, swapped(w_out, "var", 1), out_first, out_second]
        out_pieces += [swapped(out_first, "var", 1), swapped(out_second, "var", 1)]
        out_places = [var_place * out_rows, (var_place ^ 1) * out_rows]
        out_places += [(var_place ^ 2) * out_rows + place * half for place in (side, 1 - side)]
        out_places += [(var_place ^ 3) * out_rows + place * half for place in (side, 1 - side)]
    else:
        out_pieces, out_places = [lax.all_gather(w_out, "var", axis=0, tiled=True)], [0]
    received = shifted(tail, "tm", 1)
    attended = attend_main(last, block_table, query, keyval)
    coefs = jnp.stack([coef_latent, coef_pred, spread, (tm_place == 0).astype(F32)])
    return finish(coefs, attended, received, latent, fresh_noise[0], out_pieces, out_places)[None]


def solution(mesh):
    placed = (
        P("var", "tm", None),
        P("var", "tm", None),
        P(),
        P("var", None),
        P(),
        P(None, "tm"),
        P("var", None),
        P("var", None),
        P("var", None),
    )
    return jax.shard_map(
        local, mesh=mesh, in_specs=placed, out_specs=P("var", "tm", None), check_vma=False
    )
```

```python
import functools
import math

import jax
import jax.numpy as jnp
from jax import lax
from jax.experimental import pallas as pl
from jax.experimental.pallas import tpu as pltpu
from jax.sharding import PartitionSpec as P

HEADS = 12
HS = 64
SEAM = 128
BLK = 128
TSTEPS = 1000
STRIDE = 200
LANES = 128

epsilon = 1e-06
MASKED = -1e30
MICROSECOND = 10**9
VMEM_LIMIT = 18 * 1024 * 1024
ALL_VMEM = 62 * 1024 * 1024

BF16 = jnp.bfloat16
F32 = jnp.float32


def plan(moment):
    return jnp.cos((moment / TSTEPS + 0.008) / 1.008 * (math.pi / 2.0)) ** 2


def coefficients(timestep):
    current = timestep[0].astype(jnp.float32)
    abar_now = plan(current)
    abar_prev = plan(current - STRIDE)
    spread = jnp.sqrt((1.0 - abar_prev) / (1.0 - abar_now) * (1.0 - abar_now / abar_prev))
    carried = jnp.sqrt((1.0 - abar_prev) * (abar_now / abar_prev - abar_now) / (1.0 - abar_now))
    coef_pred = carried - jnp.sqrt(abar_prev) * jnp.sqrt(1.0 - abar_now) / jnp.sqrt(abar_now)
    coef_latent = jnp.sqrt(abar_prev / abar_now)
    return (current, coef_latent, coef_pred, spread)


def time_waves(current, model_width):
    half_width = model_width // 2
    frequency = jnp.exp(-math.log(10000.0) * jnp.arange(half_width, dtype=jnp.float32) / half_width)
    angles = current * frequency
    return (jnp.cos(angles)[None, :], jnp.sin(angles)[None, :])


def swapped(block, axis, bit):
    route = [(i, i ^ bit) for i in range(lax.axis_size(axis))]
    return lax.ppermute(block, axis, route)


def shifted(block, axis, distance):
    devices = range(lax.axis_size(axis))
    route = [(i - distance, i) for i in devices if i - distance in devices]
    return lax.ppermute(block, axis, route)


def vmem():
    return pl.BlockSpec(memory_space=pltpu.VMEM)


def smem():
    return pl.BlockSpec(memory_space=pltpu.SMEM)


def params(limit=VMEM_LIMIT):
    return pltpu.CompilerParams(vmem_limit_bytes=limit)


def anywhere():
    return pl.BlockSpec(memory_space=pl.ANY)


def hbm():
    return pl.BlockSpec(memory_space=pltpu.HBM)


def in_hbm(value):
    return pltpu.with_memory_space_constraint(value, pltpu.HBM)


def cost(flops):
    return pl.CostEstimate(flops=flops, bytes_accessed=1, transcendentals=0)


def whole_rows(row):
    tm_count = lax.axis_size("tm")
    sent = jnp.broadcast_to(row, (tm_count, row.shape[1]))
    arrived = lax.all_to_all(sent, "tm", 0, 0, tiled=True)
    if row.shape[1] % HS or tm_count % 8:
        arrived = arrived.reshape(1, tm_count * row.shape[1])
    return arrived


def pool_kernel(ids_ref, table_ref, after_ref, pooled_ref, columns, sem):
    del after_ref
    whole = pltpu.make_async_copy(table_ref, columns, sem)
    whole.start()
    lane = lax.broadcasted_iota(jnp.int32, (1, LANES), 1)
    whole.wait()

    def body(j, total):
        token = ids_ref[0, j]
        start = pl.multiple_of((token >> 7) * LANES, LANES)
        block = columns[:, pl.ds(start, LANES)].astype(F32)
        return total + jnp.where(lane == (token & (LANES - 1)), block, 0.0)

    count = ids_ref.shape[1]
    total = lax.fori_loop(0, count, body, jnp.zeros((columns.shape[0], LANES), F32), unroll=8)
    ones = jnp.full((8, LANES), 1.0 / count, F32)
    pooled_ref[...] = lax.dot_general(
        ones,
        total,
        (((1,), (1,)), ((), ())),
        precision=lax.Precision.HIGHEST,
        preferred_element_type=F32,
    )


def pool(prompt_ids, prompt_table, after):
    table_columns = prompt_table.T
    return pl.pallas_call(
        pool_kernel,
        out_shape=jax.ShapeDtypeStruct((8, table_columns.shape[0]), F32),
        in_specs=[smem(), hbm(), anywhere()],
        out_specs=vmem(),
        scratch_shapes=[pltpu.VMEM(table_columns.shape, BF16), pltpu.SemaphoreType.DMA],
        compiler_params=params(),
        cost_estimate=cost(1),
        name="pool_prompt",
    )(prompt_ids, in_hbm(table_columns), after)


def first_kernel(
    places_ref, query_ref, keyval_ref, out_weights_ref, latent_ref, halo_ref, out_cut_ref, *refs
):
    *cut_refs, sems = refs
    head_width = query_ref.shape[1]
    copies = [
        pltpu.make_async_copy(latent_ref.at[: halo_ref.shape[0], :], halo_ref, sems.at[0]),
    ]
    out_rows = out_cut_ref.shape[0]
    at = pl.ds(aligned(places_ref[0] * out_rows, 16), out_rows)
    copies.append(pltpu.make_async_copy(out_weights_ref.at[at, :], out_cut_ref, sems.at[1]))
    for k, target in enumerate(cut_refs):
        rows = target.shape[0]
        at = pl.ds(aligned(places_ref[1 + k] * rows, 16), rows)
        copies += [
            pltpu.make_async_copy(
                query_ref.at[at, :], target.at[:, :head_width], sems.at[2 + 2 * k]
            ),
            pltpu.make_async_copy(
                keyval_ref.at[at, :], target.at[:, head_width:], sems.at[3 + 2 * k]
            ),
        ]
    for copy in copies:
        copy.start()
    for copy in copies:
        copy.wait()


def first_rows(side, places, w_query, w_keyval, w_out, latent):
    quarter = w_query.shape[0] // 4
    columns = w_query.shape[1] + w_keyval.shape[1]
    return pl.pallas_call(
        first_kernel,
        out_shape=[
            jax.ShapeDtypeStruct((SEAM, latent.shape[1]), BF16),
            jax.ShapeDtypeStruct((w_out.shape[0] // 2, w_out.shape[1]), BF16),
        ]
        + [jax.ShapeDtypeStruct((quarter, columns), BF16)] * len(places),
        in_specs=[smem()] + [hbm()] * 4,
        out_specs=[vmem()] * (2 + len(places)),
        scratch_shapes=[pltpu.SemaphoreType.DMA((2 + 2 * len(places),))],
        compiler_params=params(),
        cost_estimate=cost(1),
        name="first_rows",
    )(
        numbers(side, *places),
        *[in_hbm(value) for value in (w_query, w_keyval, w_out, latent)],
    )


def joined(parts):
    return parts[0] if len(parts) == 1 else jnp.concatenate(parts, axis=1)


def can_route(rows):
    return lax.axis_size("var") == 4 and lax.axis_size("tm") % 4 == 0 and rows % 128 == 0


def cut(weights, which, count):
    rows = weights[0].shape[0] // count
    return joined([lax.dynamic_slice_in_dim(w, which * rows, rows, 0) for w in weights])


def gate_kernel(*refs):
    del refs


def together(*values, limit=VMEM_LIMIT):
    return pl.pallas_call(
        gate_kernel,
        out_shape=[jax.ShapeDtypeStruct(v.shape, v.dtype) for v in values],
        in_specs=[anywhere()] * len(values),
        out_specs=[anywhere()] * len(values),
        input_output_aliases={k: k for k in range(len(values))},
        compiler_params=params(limit),
        cost_estimate=cost(1),
        name="gate",
    )(*values)


def numbers(*values):
    return jnp.stack([jnp.asarray(value, jnp.int32) for value in values])


def aligned(value, multiple):
    return pl.multiple_of(value, multiple)


def scale_of(rows_ref, cos_ref, sin_ref):
    rows = rows_ref[...]
    row = jnp.concatenate([rows[k : k + 1, :] for k in range(rows.shape[0])], axis=1)
    return 1.0 + (jnp.concatenate([cos_ref[...], sin_ref[...]], axis=1) + row)


def bias_of(table_ref, last, query_block):
    blocks = table_ref.shape[0]
    biases = []
    for j in range(blocks):
        allowed = table_ref[query_block, j] > 0
        if j == blocks - 1:
            allowed = jnp.logical_and(allowed, last == 0)
        biases.append(jnp.where(allowed, 0.0, MASKED))
    return biases


def normalize(target, begin, ref, scale, width):
    for row in range(0, ref.shape[0], 32):
        values = ref[row : row + 32, :].astype(F32)
        inv_norm = lax.rsqrt(jnp.sum(values * values, axis=-1, keepdims=True) / width + epsilon)
        target[begin + row : begin + row + 32, :] = (values * inv_norm * scale).astype(BF16)


def normalize_kernel(
    latent_ref, halo_ref, rows_ref, cos_ref, sin_ref, normed_ref, window, normed, rows, sems
):
    main_rows = latent_ref.shape[0]
    copies = [
        pltpu.make_async_copy(latent_ref, window.at[:main_rows, :], sems.at[0]),
        pltpu.make_async_copy(halo_ref, window.at[main_rows:, :], sems.at[1]),
        pltpu.make_async_copy(rows_ref, rows, sems.at[2]),
    ]
    for copy in copies:
        copy.start()
    for copy in copies:
        copy.wait()
    normalize(normed, 0, window, scale_of(rows, cos_ref, sin_ref), window.shape[1])
    copy = pltpu.make_async_copy(normed, normed_ref, sems.at[3])
    copy.start()
    copy.wait()


def normalized(latent, halo, rows, waves):
    shape = (latent.shape[0] + SEAM, latent.shape[1])
    return pl.pallas_call(
        normalize_kernel,
        out_shape=pltpu.HBM(shape, BF16),
        in_specs=[hbm()] * 3 + [vmem()] * 2,
        out_specs=hbm(),
        scratch_shapes=[
            pltpu.VMEM(shape, BF16),
            pltpu.VMEM(shape, BF16),
            pltpu.VMEM(rows.shape, F32),
            pltpu.SemaphoreType.DMA((4,)),
        ],
        compiler_params=params(),
        cost_estimate=cost(MICROSECOND),
        name="normalize",
    )(in_hbm(latent), in_hbm(halo), in_hbm(rows), *waves)


def attend_rows(query, keyval_ref, bias, own_block, pair):
    head_width = keyval_ref.shape[1] // 2
    key_rows = keyval_ref.shape[0]
    blocks = len(bias)
    at = pl.ds(pair * LANES, LANES)
    value_at = pl.ds(head_width + pair * LANES, LANES)
    left = lax.broadcasted_iota(jnp.int32, (1, LANES), 1) < HS
    zero = jnp.zeros((), BF16)
    query = query * BF16(1.0 / math.sqrt(HS))
    both = jnp.concatenate([jnp.where(left, query, zero), jnp.where(left, zero, query)], axis=0)
    scores = lax.dot_general(
        both, keyval_ref[:, at], (((1,), (1,)), ((), ())), preferred_element_type=F32
    )
    cut_block = lambda j: scores[:, j * BLK : (j + 1) * BLK]
    peak = None
    for j in range(blocks):
        top = jnp.maximum(cut_block(j), cut_block(blocks + j))
        if j not in (0, own_block):
            top = top + bias[j]
        peak = top if peak is None else jnp.maximum(peak, top)
    peak = jnp.max(peak, axis=-1, keepdims=True)
    offsets = [peak if j in (0, own_block) else peak - bias[j] for j in range(blocks)]
    weights = jnp.concatenate(
        [jnp.exp(cut_block(j) - offsets[j % blocks]).astype(BF16) for j in range(2 * blocks)],
        axis=1,
    )
    ones = jnp.ones((key_rows, LANES), BF16)
    values = jnp.concatenate([keyval_ref[:, value_at], ones], axis=1)
    total = jnp.dot(weights, values, preferred_element_type=F32)
    mixed = total[:, :LANES] / total[:, LANES:]
    return jnp.where(left, mixed[:BLK], mixed[BLK:])


def project_kernel(n_wide, n_pairs, n_sources, places_ref, table_ref, normed_hbm, *refs):
    wide_pieces, refs = refs[:n_wide], refs[n_wide:]
    query_pieces, refs = refs[:n_pairs], refs[n_pairs:]
    keyval_pieces, refs = refs[:n_pairs], refs[n_pairs:]
    sources, refs = refs[:n_sources], refs[n_sources:]
    query_ref, keyval_ref, tail_ref, query_weights, keyval_weights, normed, tail_query, sems = refs
    head_width = query_weights.shape[1]
    window_rows = normed.shape[0] // 2
    main_rows = window_rows - SEAM
    own_rows = pl.ds(0, window_rows)
    source_rows = pl.ds(window_rows, window_rows)
    choice, last = places_ref[0], places_ref[1]

    rows_of = [(places_ref[2 + n_wide + k], p.shape[0]) for k, p in enumerate(query_pieces)]
    rows_of += [(places_ref[2 + k], p.shape[0]) for k, p in enumerate(wide_pieces)]
    rows_of = [pl.ds(aligned(start, 16), count) for start, count in rows_of]
    query_parts = list(query_pieces) + [p.at[:, :head_width] for p in wide_pieces]
    keyval_parts = list(keyval_pieces) + [p.at[:, head_width:] for p in wide_pieces]
    copies = [(normed_hbm, normed.at[own_rows, :])]
    copies += [(p, query_weights.at[at, :]) for p, at in zip(query_parts, rows_of)]
    copies += [(p, keyval_weights.at[at, :]) for p, at in zip(keyval_parts, rows_of)]
    copies = [
        pltpu.make_async_copy(source, target, sems.at[k])
        for k, (source, target) in enumerate(copies)
    ]
    for copy in copies:
        copy.start()
    source_copies = [
        pltpu.make_async_copy(source, normed.at[source_rows, :], sems.at[len(copies)])
        for source in sources
    ]
    for k, copy in enumerate(source_copies):
        pl.when(choice == k)(copy.start)
    for copy in copies[: 1 + len(rows_of)]:
        copy.wait()
    step = 256
    for begin in range(0, head_width, step):
        at = pl.ds(begin, step)
        result = jnp.dot(
            normed[own_rows, :], query_weights[:, at], preferred_element_type=F32
        ).astype(BF16)
        query_ref[:, at] = result[:main_rows]
        tail_query[:, at] = result[main_rows:]
    for k, copy in enumerate(source_copies):
        pl.when(choice == k)(copy.wait)
    for copy in copies[1 + len(rows_of) :]:
        copy.wait()
    for begin in range(0, 2 * head_width, step):
        at = pl.ds(begin, step)
        keyval_ref[:, at] = jnp.dot(
            normed[...], keyval_weights[:, at], preferred_element_type=F32
        ).astype(BF16)
    blocks = window_rows // BLK
    row = lax.broadcasted_iota(jnp.int32, (BLK, 1), 0).astype(F32)
    fade = 1.0 - (row + 0.5) / SEAM
    bias = bias_of(table_ref, last, blocks - 1)
    for pair in range(HEADS // 2):
        at = pl.ds(pair * LANES, LANES)
        mixed = attend_rows(tail_query[:, at], keyval_ref, bias, blocks - 1, pair)
        tail_ref[:, at] = (mixed * fade).astype(BF16)


def project(
    choice, last, block_table, normed, wide, wide_places, queries, keyvals, pair_places, sources
):
    window_rows, width = normed.shape
    keyval_width = keyvals[0].shape[1]
    head_width = keyval_width // 2
    n_copies = 1 + 2 * (len(wide) + len(queries))
    arrays = (normed, *wide, *queries, *keyvals, *sources)
    late = (*wide[6:], sources[-1])
    specs = [anywhere() if any(a is b for b in late) else hbm() for a in arrays]
    arrays = [a if any(a is b for b in late) else in_hbm(a) for a in arrays]
    return pl.pallas_call(
        functools.partial(project_kernel, len(wide), len(queries), len(sources)),
        out_shape=[
            jax.ShapeDtypeStruct((window_rows - SEAM, head_width), BF16),
            jax.ShapeDtypeStruct((2 * window_rows, keyval_width), BF16),
            jax.ShapeDtypeStruct((SEAM, head_width), BF16),
        ],
        in_specs=[smem(), smem()] + specs,
        out_specs=[vmem()] * 3,
        scratch_shapes=[
            pltpu.VMEM((width, head_width), BF16),
            pltpu.VMEM((width, keyval_width), BF16),
            pltpu.VMEM((2 * window_rows, width), BF16),
            pltpu.VMEM((SEAM, head_width), BF16),
            pltpu.SemaphoreType.DMA((n_copies + 1,)),
        ],
        compiler_params=params(),
        cost_estimate=cost(10 * MICROSECOND),
        name="project_attend_tail",
    )(
        numbers(choice, last, *wide_places, *pair_places),
        block_table,
        *arrays,
    )


def main_kernel(places_ref, table_ref, query_ref, keyval_ref, out_ref):
    blocks = keyval_ref.shape[0] // (2 * BLK)
    for i in range(blocks - 1):
        bias = bias_of(table_ref, places_ref[0], i)
        rows = pl.ds(i * BLK, BLK)
        for pair in range(HEADS // 2):
            at = pl.ds(pair * LANES, LANES)
            out_ref[rows, at] = attend_rows(query_ref[rows, at], keyval_ref, bias, i, pair)


def attend_main(last, block_table, query, keyval):
    rows, width = query.shape
    return pl.pallas_call(
        main_kernel,
        out_shape=jax.ShapeDtypeStruct((rows, width), F32),
        in_specs=[smem(), smem(), vmem(), vmem()],
        out_specs=vmem(),
        compiler_params=params(),
        cost_estimate=cost(4 * MICROSECOND),
        name="attend_main",
    )(numbers(last), block_table, query, keyval)


def finish_kernel(
    n_pieces, places_ref, coef_ref, attended_ref, received_ref, latent_ref, noise_ref, *refs
):
    pieces, (out_ref, weights) = refs[:n_pieces], refs[n_pieces:]
    for k, piece in enumerate(pieces):
        weights[pl.ds(aligned(places_ref[k], 16), piece.shape[0]), :] = piece[...]
    row = lax.broadcasted_iota(jnp.int32, (SEAM, 1), 0).astype(F32)
    ramp_up = jnp.where(coef_ref[3] > 0.5, 1.0, (row + 0.5) / SEAM)
    lead = attended_ref[:SEAM, :] * ramp_up + received_ref[...].astype(F32)
    blended = jnp.concatenate([lead, attended_ref[SEAM:, :]], axis=0).astype(BF16)
    step = 256
    for begin in range(0, out_ref.shape[1], step):
        at = pl.ds(begin, step)
        prediction = jnp.dot(blended, weights[:, at], preferred_element_type=F32)
        result = (
            coef_ref[0] * latent_ref[:, at].astype(F32)
            + coef_ref[1] * prediction
            + coef_ref[2] * noise_ref[:, at].astype(F32)
        )
        out_ref[:, at] = result.astype(BF16)


def finish(coefs, attended, received, latent, noise, pieces, places):
    return pl.pallas_call(
        functools.partial(finish_kernel, len(pieces)),
        out_shape=jax.ShapeDtypeStruct(latent.shape, BF16),
        in_specs=[smem(), smem()] + [vmem()] * (4 + len(pieces)),
        out_specs=vmem(),
        scratch_shapes=[pltpu.VMEM((attended.shape[1], latent.shape[1]), BF16)],
        compiler_params=params(),
        cost_estimate=cost(3 * MICROSECOND),
        name="blend_and_step",
    )(
        numbers(*places),
        coefs,
        attended,
        received,
        latent,
        noise,
        *pieces,
    )


def from_source(value):
    bits = []
    bit = lax.axis_size("var") // 2
    while bit:
        bits.append(bit)
        bit //= 2
    return [(lax.ppermute(value, "var", [(0, bit)]), bit) for bit in bits]


def passed_on(value, arrivals):
    count = lax.axis_size("var")
    place = lax.axis_index("var")
    arrays, choice = [value, arrivals[0][0]], (place == arrivals[0][1]).astype(jnp.int32)
    for array, bit in arrivals[1:]:
        payload = functools.reduce(jnp.add, arrays[1:])
        route = [(i, i + bit) for i in range(2 * bit, count, 2 * bit)]
        choice = jnp.where(place == bit, len(arrays), choice)
        arrays.append(array)
        choice = jnp.where((place > bit) & (place % (2 * bit) == bit), len(arrays), choice)
        arrays.append(lax.ppermute(payload, "var", route))
    return arrays, choice


def local(
    latent, fresh_noise, timestep, prompt_ids, block_table, prompt_table, w_query, w_keyval, w_out
):
    latent = latent[0]
    own_rows, model_width = latent.shape
    tm_count = lax.axis_size("tm")
    tm_place = lax.axis_index("tm")
    var_place = lax.axis_index("var")
    rows = w_query.shape[0]
    routed = can_route(rows)
    corner = tm_place & 3

    side = tm_place & 1
    halo_rows, out_cut, *cuts = first_rows(
        side if routed else 0,
        (corner, corner ^ 3) if routed else (),
        w_query,
        w_keyval,
        w_out,
        latent,
    )
    pooled = pool(prompt_ids, prompt_table, halo_rows)
    halo = shifted(halo_rows, "tm", -1)
    pooled = whole_rows(pooled[:1])
    if routed:
        quarter = rows // 4
        first = swapped(cuts[0], "var", 2)
        fourth = swapped(cuts[1], "var", 2)
        halo, pooled, first, fourth = together(
            halo, pooled, first, fourth, limit=ALL_VMEM
        )

    current, coef_latent, coef_pred, spread = coefficients(timestep)
    normed = normalized(latent, halo, pooled, time_waves(current, model_width))
    sources = from_source(normed)
    if routed:
        second = swapped(first, "tm", 1)
        third = swapped(first, "tm", 2)
        queries, keyvals = [w_query], [w_keyval]
        fetched = [second, third]
        fetched += [swapped(piece, "var", 1) for piece in (first, fourth, w_query, w_keyval)]
        fetched += [swapped(out_cut, "var", 2)] + [array for array, _ in sources]
        second, third, first_over, fourth_over, partner_query, partner_keyval, *fetched = together(
            *fetched, limit=ALL_VMEM
        )
        out_first, *fetched = fetched
        sources = [(array, bit) for array, (_, bit) in zip(fetched, sources)]

        wide = [first, second, third, fourth, first_over, fourth_over]
        wide += [swapped(second, "var", 1), swapped(third, "var", 1)]
        here, there = (var_place ^ 2) * rows, (var_place ^ 3) * rows
        wide_places = [here + (corner ^ k) * quarter for k in range(4)]
        wide_places += [there + (corner ^ k) * quarter for k in (0, 3, 1, 2)]
        queries, keyvals = [w_query, partner_query], [w_keyval, partner_keyval]
        pair_places = [var_place * rows, (var_place ^ 1) * rows]
    else:
        wide, wide_places, pair_places = [], [], [0]
        queries = [lax.all_gather(w_query, "var", axis=0, tiled=True)]
        keyvals = [lax.all_gather(w_keyval, "var", axis=0, tiled=True)]
    sources, choice = passed_on(normed, sources)
    last = tm_place == tm_count - 1
    query, keyval, tail = project(
        choice,
        last,
        block_table,
        normed,
        wide,
        wide_places,
        queries,
        keyvals,
        pair_places,
        sources,
    )
    if routed:
        tail, out_second = together(tail, swapped(out_first, "tm", 1))
        out_rows = w_out.shape[0]
        half = out_rows // 2
        out_pieces = [w_out, swapped(w_out, "var", 1), out_first, out_second]
        out_pieces += [swapped(out_first, "var", 1), swapped(out_second, "var", 1)]
        out_places = [var_place * out_rows, (var_place ^ 1) * out_rows]
        out_places += [(var_place ^ 2) * out_rows + place * half for place in (side, 1 - side)]
        out_places += [(var_place ^ 3) * out_rows + place * half for place in (side, 1 - side)]
    else:
        out_pieces, out_places = [lax.all_gather(w_out, "var", axis=0, tiled=True)], [0]
    received = shifted(tail, "tm", 1)
    attended = attend_main(last, block_table, query, keyval)
    coefs = jnp.stack([coef_latent, coef_pred, spread, (tm_place == 0).astype(F32)])
    return finish(coefs, attended, received, latent, fresh_noise[0], out_pieces, out_places)[None]


def solution(mesh):
    placed = (
        P("var", "tm", None),
        P("var", "tm", None),
        P(),
        P("var", None),
        P(),
        P(None, "tm"),
        P("var", None),
        P("var", None),
        P("var", None),
    )
    return jax.shard_map(
        local, mesh=mesh, in_specs=placed, out_specs=P("var", "tm", None), check_vma=False
    )
```

```python
import functools
import math

import jax
import jax.numpy as jnp
from jax import lax
from jax.experimental import pallas as pl
from jax.experimental.pallas import tpu as pltpu
from jax.sharding import PartitionSpec as P

HEADS = 12
HS = 64
SEAM = 128
BLK = 128
TSTEPS = 1000
STRIDE = 200
LANES = 128

epsilon = 1e-06
MASKED = -1e30
MICROSECOND = 10**9
VMEM_LIMIT = 18 * 1024 * 1024
ALL_VMEM = 62 * 1024 * 1024

BF16 = jnp.bfloat16
F32 = jnp.float32


def plan(moment):
    return jnp.cos((moment / TSTEPS + 0.008) / 1.008 * (math.pi / 2.0)) ** 2


def coefficients(timestep):
    current = timestep[0].astype(jnp.float32)
    abar_now = plan(current)
    abar_prev = plan(current - STRIDE)
    spread = jnp.sqrt((1.0 - abar_prev) / (1.0 - abar_now) * (1.0 - abar_now / abar_prev))
    carried = jnp.sqrt((1.0 - abar_prev) * (abar_now / abar_prev - abar_now) / (1.0 - abar_now))
    coef_pred = carried - jnp.sqrt(abar_prev) * jnp.sqrt(1.0 - abar_now) / jnp.sqrt(abar_now)
    coef_latent = jnp.sqrt(abar_prev / abar_now)
    return (current, coef_latent, coef_pred, spread)


def time_waves(current, model_width):
    half_width = model_width // 2
    frequency = jnp.exp(-math.log(10000.0) * jnp.arange(half_width, dtype=jnp.float32) / half_width)
    angles = current * frequency
    return (jnp.cos(angles)[None, :], jnp.sin(angles)[None, :])


def swapped(block, axis, bit):
    route = [(i, i ^ bit) for i in range(lax.axis_size(axis))]
    return lax.ppermute(block, axis, route)


def shifted(block, axis, distance):
    devices = range(lax.axis_size(axis))
    route = [(i - distance, i) for i in devices if i - distance in devices]
    return lax.ppermute(block, axis, route)


def vmem():
    return pl.BlockSpec(memory_space=pltpu.VMEM)


def smem():
    return pl.BlockSpec(memory_space=pltpu.SMEM)


def params(limit=VMEM_LIMIT):
    return pltpu.CompilerParams(vmem_limit_bytes=limit)


def anywhere():
    return pl.BlockSpec(memory_space=pl.ANY)


def hbm():
    return pl.BlockSpec(memory_space=pltpu.HBM)


def in_hbm(value):
    return pltpu.with_memory_space_constraint(value, pltpu.HBM)


def cost(flops):
    return pl.CostEstimate(flops=flops, bytes_accessed=1, transcendentals=0)


def whole_rows(row):
    tm_count = lax.axis_size("tm")
    sent = row if row.shape[0] == tm_count else jnp.broadcast_to(row[:1], (tm_count, row.shape[1]))
    arrived = lax.all_to_all(sent, "tm", 0, 0, tiled=True)
    if row.shape[1] % HS or tm_count % 8:
        arrived = arrived.reshape(1, tm_count * row.shape[1])
    return arrived


def pool_kernel(ids_ref, table_ref, after_ref, pooled_ref, columns, sem):
    del after_ref
    whole = pltpu.make_async_copy(table_ref, columns, sem)
    whole.start()
    lane = lax.broadcasted_iota(jnp.int32, (1, LANES), 1)
    whole.wait()

    def body(j, total):
        token = ids_ref[0, j]
        start = pl.multiple_of((token >> 7) * LANES, LANES)
        block = columns[:, pl.ds(start, LANES)].astype(F32)
        return total + jnp.where(lane == (token & (LANES - 1)), block, 0.0)

    count = ids_ref.shape[1]
    total = lax.fori_loop(0, count, body, jnp.zeros((columns.shape[0], LANES), F32), unroll=8)
    ones = jnp.full((8, LANES), 1.0 / count, F32)
    pooled_ref[...] = lax.dot_general(
        ones,
        total,
        (((1,), (1,)), ((), ())),
        precision=lax.Precision.HIGHEST,
        preferred_element_type=F32,
    )


def pool(prompt_ids, prompt_table, after):
    table_columns = prompt_table.T
    return pl.pallas_call(
        pool_kernel,
        out_shape=jax.ShapeDtypeStruct((8, table_columns.shape[0]), F32),
        in_specs=[smem(), hbm(), anywhere()],
        out_specs=vmem(),
        scratch_shapes=[pltpu.VMEM(table_columns.shape, BF16), pltpu.SemaphoreType.DMA],
        compiler_params=params(),
        cost_estimate=cost(1),
        name="pool_prompt",
    )(prompt_ids, in_hbm(table_columns), after)


def first_kernel(
    places_ref, query_ref, keyval_ref, out_weights_ref, latent_ref, halo_ref, out_cut_ref, *refs
):
    *cut_refs, sems = refs
    head_width = query_ref.shape[1]
    copies = [
        pltpu.make_async_copy(latent_ref.at[: halo_ref.shape[0], :], halo_ref, sems.at[0]),
    ]
    out_rows = out_cut_ref.shape[0]
    at = pl.ds(aligned(places_ref[0] * out_rows, 16), out_rows)
    copies.append(pltpu.make_async_copy(out_weights_ref.at[at, :], out_cut_ref, sems.at[1]))
    for k, target in enumerate(cut_refs):
        rows = target.shape[0]
        at = pl.ds(aligned(places_ref[1 + k] * rows, 16), rows)
        copies += [
            pltpu.make_async_copy(
                query_ref.at[at, :], target.at[:, :head_width], sems.at[2 + 2 * k]
            ),
            pltpu.make_async_copy(
                keyval_ref.at[at, :], target.at[:, head_width:], sems.at[3 + 2 * k]
            ),
        ]
    for copy in copies:
        copy.start()
    for copy in copies:
        copy.wait()


def first_rows(side, places, w_query, w_keyval, w_out, latent):
    quarter = w_query.shape[0] // 4
    columns = w_query.shape[1] + w_keyval.shape[1]
    return pl.pallas_call(
        first_kernel,
        out_shape=[
            jax.ShapeDtypeStruct((SEAM, latent.shape[1]), BF16),
            jax.ShapeDtypeStruct((w_out.shape[0] // 2, w_out.shape[1]), BF16),
        ]
        + [jax.ShapeDtypeStruct((quarter, columns), BF16)] * len(places),
        in_specs=[smem()] + [hbm()] * 4,
        out_specs=[vmem()] * (2 + len(places)),
        scratch_shapes=[pltpu.SemaphoreType.DMA((2 + 2 * len(places),))],
        compiler_params=params(),
        cost_estimate=cost(1),
        name="first_rows",
    )(
        numbers(side, *places),
        *[in_hbm(value) for value in (w_query, w_keyval, w_out, latent)],
    )


def joined(parts):
    return parts[0] if len(parts) == 1 else jnp.concatenate(parts, axis=1)


def can_route(rows):
    return lax.axis_size("var") == 4 and lax.axis_size("tm") % 4 == 0 and rows % 128 == 0


def cut(weights, which, count):
    rows = weights[0].shape[0] // count
    return joined([lax.dynamic_slice_in_dim(w, which * rows, rows, 0) for w in weights])


def gate_kernel(*refs):
    del refs


def together(*values, limit=VMEM_LIMIT):
    return pl.pallas_call(
        gate_kernel,
        out_shape=[jax.ShapeDtypeStruct(v.shape, v.dtype) for v in values],
        in_specs=[anywhere()] * len(values),
        out_specs=[anywhere()] * len(values),
        input_output_aliases={k: k for k in range(len(values))},
        compiler_params=params(limit),
        cost_estimate=cost(1),
        name="gate",
    )(*values)


def numbers(*values):
    return jnp.stack([jnp.asarray(value, jnp.int32) for value in values])


def aligned(value, multiple):
    return pl.multiple_of(value, multiple)


def scale_of(rows_ref, cos_ref, sin_ref):
    rows = rows_ref[...]
    row = jnp.concatenate([rows[k : k + 1, :] for k in range(rows.shape[0])], axis=1)
    return 1.0 + (jnp.concatenate([cos_ref[...], sin_ref[...]], axis=1) + row)


def bias_of(table_ref, last, query_block):
    blocks = table_ref.shape[0]
    biases = []
    for j in range(blocks):
        allowed = table_ref[query_block, j] > 0
        if j == blocks - 1:
            allowed = jnp.logical_and(allowed, last == 0)
        biases.append(jnp.where(allowed, 0.0, MASKED))
    return biases


def normalize(target, begin, ref, scale, width):
    for row in range(0, ref.shape[0], 32):
        values = ref[row : row + 32, :].astype(F32)
        inv_norm = lax.rsqrt(jnp.sum(values * values, axis=-1, keepdims=True) / width + epsilon)
        target[begin + row : begin + row + 32, :] = (values * inv_norm * scale).astype(BF16)


def normalize_kernel(
    latent_ref, halo_ref, rows_ref, cos_ref, sin_ref, normed_ref, window, normed, rows, sems
):
    main_rows = latent_ref.shape[0]
    part = SEAM
    parts = [pl.ds(begin, part) for begin in range(0, window.shape[0], part)]
    sources = [latent_ref.at[at, :] for at in parts[: main_rows // part]] + [halo_ref]
    copies = [pltpu.make_async_copy(rows_ref, rows, sems.at[0])]
    copies += [
        pltpu.make_async_copy(source, window.at[at, :], sems.at[1 + k])
        for k, (source, at) in enumerate(zip(sources, parts))
    ]
    for copy in copies:
        copy.start()
    copies[0].wait()
    scale = scale_of(rows, cos_ref, sin_ref)
    stores = []
    for k, at in enumerate(parts):
        copies[1 + k].wait()
        normalize(normed.at[at, :], 0, window.at[at, :], scale, window.shape[1])
        store = pltpu.make_async_copy(
            normed.at[at, :], normed_ref.at[at, :], sems.at[1 + len(parts) + k]
        )
        store.start()
        stores.append(store)
    for store in stores:
        store.wait()


def normalized(latent, halo, rows, waves):
    shape = (latent.shape[0] + SEAM, latent.shape[1])
    return pl.pallas_call(
        normalize_kernel,
        out_shape=pltpu.HBM(shape, BF16),
        in_specs=[hbm()] * 3 + [vmem()] * 2,
        out_specs=hbm(),
        scratch_shapes=[
            pltpu.VMEM(shape, BF16),
            pltpu.VMEM(shape, BF16),
            pltpu.VMEM(rows.shape, F32),
            pltpu.SemaphoreType.DMA((1 + 2 * (shape[0] // SEAM),)),
        ],
        compiler_params=params(),
        cost_estimate=cost(MICROSECOND),
        name="normalize",
    )(in_hbm(latent), in_hbm(halo), in_hbm(rows), *waves)


def attend_rows(query, keyval_ref, bias, own_block, pair):
    head_width = keyval_ref.shape[1] // 2
    key_rows = keyval_ref.shape[0]
    blocks = len(bias)
    at = pl.ds(pair * LANES, LANES)
    value_at = pl.ds(head_width + pair * LANES, LANES)
    left = lax.broadcasted_iota(jnp.int32, (1, LANES), 1) < HS
    zero = jnp.zeros((), BF16)
    query = query * BF16(1.0 / math.sqrt(HS))
    both = jnp.concatenate([jnp.where(left, query, zero), jnp.where(left, zero, query)], axis=0)
    scores = lax.dot_general(
        both, keyval_ref[:, at], (((1,), (1,)), ((), ())), preferred_element_type=F32
    )
    cut_block = lambda j: scores[:, j * BLK : (j + 1) * BLK]
    peak = None
    for j in range(blocks):
        top = jnp.maximum(cut_block(j), cut_block(blocks + j))
        if j not in (0, own_block):
            top = top + bias[j]
        peak = top if peak is None else jnp.maximum(peak, top)
    peak = jnp.max(peak, axis=-1, keepdims=True)
    offsets = [peak if j in (0, own_block) else peak - bias[j] for j in range(blocks)]
    weights = jnp.concatenate(
        [jnp.exp(cut_block(j) - offsets[j % blocks]).astype(BF16) for j in range(2 * blocks)],
        axis=1,
    )
    ones = jnp.ones((key_rows, LANES), BF16)
    values = jnp.concatenate([keyval_ref[:, value_at], ones], axis=1)
    total = jnp.dot(weights, values, preferred_element_type=F32)
    mixed = total[:, :LANES] / total[:, LANES:]
    return jnp.where(left, mixed[:BLK], mixed[BLK:])


def project_kernel(n_wide, n_pairs, n_sources, places_ref, table_ref, normed_hbm, *refs):
    wide_pieces, refs = refs[:n_wide], refs[n_wide:]
    query_pieces, refs = refs[:n_pairs], refs[n_pairs:]
    keyval_pieces, refs = refs[:n_pairs], refs[n_pairs:]
    sources, refs = refs[:n_sources], refs[n_sources:]
    query_ref, keyval_ref, tail_ref, query_weights, keyval_weights, normed, tail_query, sems = refs
    head_width = query_weights.shape[1]
    window_rows = normed.shape[0] // 2
    main_rows = window_rows - SEAM
    own_rows = pl.ds(0, window_rows)
    source_rows = pl.ds(window_rows, window_rows)
    choice, last = places_ref[0], places_ref[1]

    rows_of = [(places_ref[2 + n_wide + k], p.shape[0]) for k, p in enumerate(query_pieces)]
    rows_of += [(places_ref[2 + k], p.shape[0]) for k, p in enumerate(wide_pieces)]
    rows_of = [pl.ds(aligned(start, 16), count) for start, count in rows_of]
    query_parts = list(query_pieces) + [p.at[:, :head_width] for p in wide_pieces]
    keyval_parts = list(keyval_pieces) + [p.at[:, head_width:] for p in wide_pieces]
    copies = [(normed_hbm, normed.at[own_rows, :])]
    copies += [(p, query_weights.at[at, :]) for p, at in zip(query_parts, rows_of)]
    copies += [(p, keyval_weights.at[at, :]) for p, at in zip(keyval_parts, rows_of)]
    copies = [
        pltpu.make_async_copy(source, target, sems.at[k])
        for k, (source, target) in enumerate(copies)
    ]
    for copy in copies:
        copy.start()
    source_copies = [
        pltpu.make_async_copy(source, normed.at[source_rows, :], sems.at[len(copies)])
        for source in sources
    ]
    for k, copy in enumerate(source_copies):
        pl.when(choice == k)(copy.start)
    for copy in copies[: 1 + len(rows_of)]:
        copy.wait()
    step = 256
    for begin in range(0, head_width, step):
        at = pl.ds(begin, step)
        result = jnp.dot(
            normed[own_rows, :], query_weights[:, at], preferred_element_type=F32
        ).astype(BF16)
        query_ref[:, at] = result[:main_rows]
        tail_query[:, at] = result[main_rows:]
    for k, copy in enumerate(source_copies):
        pl.when(choice == k)(copy.wait)
    for copy in copies[1 + len(rows_of) :]:
        copy.wait()
    for begin in range(0, 2 * head_width, step):
        at = pl.ds(begin, step)
        keyval_ref[:, at] = jnp.dot(
            normed[...], keyval_weights[:, at], preferred_element_type=F32
        ).astype(BF16)
    blocks = window_rows // BLK
    row = lax.broadcasted_iota(jnp.int32, (BLK, 1), 0).astype(F32)
    fade = 1.0 - (row + 0.5) / SEAM
    bias = bias_of(table_ref, last, blocks - 1)
    for pair in range(HEADS // 2):
        at = pl.ds(pair * LANES, LANES)
        mixed = attend_rows(tail_query[:, at], keyval_ref, bias, blocks - 1, pair)
        tail_ref[:, at] = (mixed * fade).astype(BF16)


def project(
    choice, last, block_table, normed, wide, wide_places, queries, keyvals, pair_places, sources
):
    window_rows, width = normed.shape
    keyval_width = keyvals[0].shape[1]
    head_width = keyval_width // 2
    n_copies = 1 + 2 * (len(wide) + len(queries))
    arrays = (normed, *wide, *queries, *keyvals, *sources)
    late = (*wide[6:], sources[-1])
    specs = [anywhere() if any(a is b for b in late) else hbm() for a in arrays]
    arrays = [a if any(a is b for b in late) else in_hbm(a) for a in arrays]
    return pl.pallas_call(
        functools.partial(project_kernel, len(wide), len(queries), len(sources)),
        out_shape=[
            jax.ShapeDtypeStruct((window_rows - SEAM, head_width), BF16),
            jax.ShapeDtypeStruct((2 * window_rows, keyval_width), BF16),
            jax.ShapeDtypeStruct((SEAM, head_width), BF16),
        ],
        in_specs=[smem(), smem()] + specs,
        out_specs=[vmem()] * 3,
        scratch_shapes=[
            pltpu.VMEM((width, head_width), BF16),
            pltpu.VMEM((width, keyval_width), BF16),
            pltpu.VMEM((2 * window_rows, width), BF16),
            pltpu.VMEM((SEAM, head_width), BF16),
            pltpu.SemaphoreType.DMA((n_copies + 1,)),
        ],
        compiler_params=params(),
        cost_estimate=cost(10 * MICROSECOND),
        name="project_attend_tail",
    )(
        numbers(choice, last, *wide_places, *pair_places),
        block_table,
        *arrays,
    )


def main_kernel(places_ref, table_ref, query_ref, keyval_ref, out_ref):
    blocks = keyval_ref.shape[0] // (2 * BLK)
    for i in range(blocks - 1):
        bias = bias_of(table_ref, places_ref[0], i)
        rows = pl.ds(i * BLK, BLK)
        for pair in range(HEADS // 2):
            at = pl.ds(pair * LANES, LANES)
            out_ref[rows, at] = attend_rows(query_ref[rows, at], keyval_ref, bias, i, pair)


def attend_main(last, block_table, query, keyval):
    rows, width = query.shape
    return pl.pallas_call(
        main_kernel,
        out_shape=jax.ShapeDtypeStruct((rows, width), F32),
        in_specs=[smem(), smem(), vmem(), vmem()],
        out_specs=vmem(),
        compiler_params=params(),
        cost_estimate=cost(4 * MICROSECOND),
        name="attend_main",
    )(numbers(last), block_table, query, keyval)


def finish_kernel(
    n_pieces, places_ref, coef_ref, attended_ref, received_ref, latent_ref, noise_ref, *refs
):
    pieces, (out_ref, weights) = refs[:n_pieces], refs[n_pieces:]
    for k, piece in enumerate(pieces):
        weights[pl.ds(aligned(places_ref[k], 16), piece.shape[0]), :] = piece[...]
    row = lax.broadcasted_iota(jnp.int32, (SEAM, 1), 0).astype(F32)
    ramp_up = jnp.where(coef_ref[3] > 0.5, 1.0, (row + 0.5) / SEAM)
    lead = attended_ref[:SEAM, :] * ramp_up + received_ref[...].astype(F32)
    blended = jnp.concatenate([lead, attended_ref[SEAM:, :]], axis=0).astype(BF16)
    step = 256
    for begin in range(0, out_ref.shape[1], step):
        at = pl.ds(begin, step)
        prediction = jnp.dot(blended, weights[:, at], preferred_element_type=F32)
        result = (
            coef_ref[0] * latent_ref[:, at].astype(F32)
            + coef_ref[1] * prediction
            + coef_ref[2] * noise_ref[:, at].astype(F32)
        )
        out_ref[:, at] = result.astype(BF16)


def finish(coefs, attended, received, latent, noise, pieces, places):
    return pl.pallas_call(
        functools.partial(finish_kernel, len(pieces)),
        out_shape=jax.ShapeDtypeStruct(latent.shape, BF16),
        in_specs=[smem(), smem()] + [vmem()] * (4 + len(pieces)),
        out_specs=vmem(),
        scratch_shapes=[pltpu.VMEM((attended.shape[1], latent.shape[1]), BF16)],
        compiler_params=params(),
        cost_estimate=cost(3 * MICROSECOND),
        name="blend_and_step",
    )(
        numbers(*places),
        coefs,
        attended,
        received,
        latent,
        noise,
        *pieces,
    )


def from_source(value):
    bits = []
    bit = lax.axis_size("var") // 2
    while bit:
        bits.append(bit)
        bit //= 2
    return [(lax.ppermute(value, "var", [(0, bit)]), bit) for bit in bits]


def passed_on(value, arrivals):
    count = lax.axis_size("var")
    place = lax.axis_index("var")
    arrays, choice = [value, arrivals[0][0]], (place == arrivals[0][1]).astype(jnp.int32)
    for array, bit in arrivals[1:]:
        payload = functools.reduce(jnp.add, arrays[1:])
        route = [(i, i + bit) for i in range(2 * bit, count, 2 * bit)]
        choice = jnp.where(place == bit, len(arrays), choice)
        arrays.append(array)
        choice = jnp.where((place > bit) & (place % (2 * bit) == bit), len(arrays), choice)
        arrays.append(lax.ppermute(payload, "var", route))
    return arrays, choice


def local(
    latent, fresh_noise, timestep, prompt_ids, block_table, prompt_table, w_query, w_keyval, w_out
):
    latent = latent[0]
    own_rows, model_width = latent.shape
    tm_count = lax.axis_size("tm")
    tm_place = lax.axis_index("tm")
    var_place = lax.axis_index("var")
    rows = w_query.shape[0]
    routed = can_route(rows)
    corner = tm_place & 3

    side = tm_place & 1
    halo_rows, out_cut, *cuts = first_rows(
        side if routed else 0,
        (corner, corner ^ 3) if routed else (),
        w_query,
        w_keyval,
        w_out,
        latent,
    )
    pooled = pool(prompt_ids, prompt_table, halo_rows)
    halo = shifted(halo_rows, "tm", -1)
    pooled = whole_rows(pooled)
    if routed:
        quarter = rows // 4
        first = swapped(cuts[0], "var", 2)
        fourth = swapped(cuts[1], "var", 2)
        halo, pooled, first, fourth = together(
            halo, pooled, first, fourth, limit=ALL_VMEM
        )

    current, coef_latent, coef_pred, spread = coefficients(timestep)
    normed = normalized(latent, halo, pooled, time_waves(current, model_width))
    sources = from_source(normed)
    if routed:
        second = swapped(first, "tm", 1)
        third = swapped(first, "tm", 2)
        queries, keyvals = [w_query], [w_keyval]
        fetched = [second, third]
        fetched += [swapped(piece, "var", 1) for piece in (first, fourth, w_query, w_keyval)]
        fetched += [swapped(out_cut, "var", 2)] + [array for array, _ in sources]
        second, third, first_over, fourth_over, partner_query, partner_keyval, *fetched = together(
            *fetched, limit=ALL_VMEM
        )
        out_first, *fetched = fetched
        sources = [(array, bit) for array, (_, bit) in zip(fetched, sources)]

        wide = [first, second, third, fourth, first_over, fourth_over]
        wide += [swapped(second, "var", 1), swapped(third, "var", 1)]
        here, there = (var_place ^ 2) * rows, (var_place ^ 3) * rows
        wide_places = [here + (corner ^ k) * quarter for k in range(4)]
        wide_places += [there + (corner ^ k) * quarter for k in (0, 3, 1, 2)]
        queries, keyvals = [w_query, partner_query], [w_keyval, partner_keyval]
        pair_places = [var_place * rows, (var_place ^ 1) * rows]
    else:
        wide, wide_places, pair_places = [], [], [0]
        queries = [lax.all_gather(w_query, "var", axis=0, tiled=True)]
        keyvals = [lax.all_gather(w_keyval, "var", axis=0, tiled=True)]
    sources, choice = passed_on(normed, sources)
    last = tm_place == tm_count - 1
    query, keyval, tail = project(
        choice,
        last,
        block_table,
        normed,
        wide,
        wide_places,
        queries,
        keyvals,
        pair_places,
        sources,
    )
    if routed:
        tail, out_second = together(tail, swapped(out_first, "tm", 1))
        out_rows = w_out.shape[0]
        half = out_rows // 2
        out_pieces = [w_out, swapped(w_out, "var", 1), out_first, out_second]
        out_pieces += [swapped(out_first, "var", 1), swapped(out_second, "var", 1)]
        out_places = [var_place * out_rows, (var_place ^ 1) * out_rows]
        out_places += [(var_place ^ 2) * out_rows + place * half for place in (side, 1 - side)]
        out_places += [(var_place ^ 3) * out_rows + place * half for place in (side, 1 - side)]
    else:
        out_pieces, out_places = [lax.all_gather(w_out, "var", axis=0, tiled=True)], [0]
    received = shifted(tail, "tm", 1)
    attended = attend_main(last, block_table, query, keyval)
    coefs = jnp.stack([coef_latent, coef_pred, spread, (tm_place == 0).astype(F32)])
    return finish(coefs, attended, received, latent, fresh_noise[0], out_pieces, out_places)[None]


def solution(mesh):
    placed = (
        P("var", "tm", None),
        P("var", "tm", None),
        P(),
        P("var", None),
        P(),
        P(None, "tm"),
        P("var", None),
        P("var", None),
        P("var", None),
    )
    return jax.shard_map(
        local, mesh=mesh, in_specs=placed, out_specs=P("var", "tm", None), check_vma=False
    )
```

```python
import functools
import math

import jax
import jax.numpy as jnp
from jax import lax
from jax.experimental import pallas as pl
from jax.experimental.pallas import tpu as pltpu
from jax.sharding import PartitionSpec as P

HEADS = 12
HS = 64
SEAM = 128
BLK = 128
TSTEPS = 1000
STRIDE = 200
LANES = 128

epsilon = 1e-06
MASKED = -1e30
MICROSECOND = 10**9
VMEM_LIMIT = 18 * 1024 * 1024
ALL_VMEM = 62 * 1024 * 1024

BF16 = jnp.bfloat16
F32 = jnp.float32


def plan(moment):
    return jnp.cos((moment / TSTEPS + 0.008) / 1.008 * (math.pi / 2.0)) ** 2


def coefficients(timestep):
    current = timestep[0].astype(jnp.float32)
    abar_now = plan(current)
    abar_prev = plan(current - STRIDE)
    spread = jnp.sqrt((1.0 - abar_prev) / (1.0 - abar_now) * (1.0 - abar_now / abar_prev))
    carried = jnp.sqrt((1.0 - abar_prev) * (abar_now / abar_prev - abar_now) / (1.0 - abar_now))
    coef_pred = carried - jnp.sqrt(abar_prev) * jnp.sqrt(1.0 - abar_now) / jnp.sqrt(abar_now)
    coef_latent = jnp.sqrt(abar_prev / abar_now)
    return (current, coef_latent, coef_pred, spread)


def time_waves(current, model_width):
    half_width = model_width // 2
    frequency = jnp.exp(-math.log(10000.0) * jnp.arange(half_width, dtype=jnp.float32) / half_width)
    angles = current * frequency
    return (jnp.cos(angles)[None, :], jnp.sin(angles)[None, :])


def swapped(block, axis, bit):
    route = [(i, i ^ bit) for i in range(lax.axis_size(axis))]
    return lax.ppermute(block, axis, route)


def shifted(block, axis, distance):
    devices = range(lax.axis_size(axis))
    route = [(i - distance, i) for i in devices if i - distance in devices]
    return lax.ppermute(block, axis, route)


def vmem():
    return pl.BlockSpec(memory_space=pltpu.VMEM)


def smem():
    return pl.BlockSpec(memory_space=pltpu.SMEM)


def params(limit=VMEM_LIMIT):
    return pltpu.CompilerParams(vmem_limit_bytes=limit)


def anywhere():
    return pl.BlockSpec(memory_space=pl.ANY)


def hbm():
    return pl.BlockSpec(memory_space=pltpu.HBM)


def in_hbm(value):
    return pltpu.with_memory_space_constraint(value, pltpu.HBM)


def cost(flops):
    return pl.CostEstimate(flops=flops, bytes_accessed=1, transcendentals=0)


def whole_rows(row):
    tm_count = lax.axis_size("tm")
    sent = row if row.shape[0] == tm_count else jnp.broadcast_to(row[:1], (tm_count, row.shape[1]))
    arrived = lax.all_to_all(sent, "tm", 0, 0, tiled=True)
    if row.shape[1] % HS or tm_count % 8:
        arrived = arrived.reshape(1, tm_count * row.shape[1])
    return arrived


def pool_kernel(ids_ref, table_ref, after_ref, pooled_ref, columns, sem):
    del after_ref
    whole = pltpu.make_async_copy(table_ref, columns, sem)
    whole.start()
    lane = lax.broadcasted_iota(jnp.int32, (1, LANES), 1)
    whole.wait()

    def body(j, total):
        token = ids_ref[0, j]
        start = pl.multiple_of((token >> 7) * LANES, LANES)
        block = columns[:, pl.ds(start, LANES)].astype(F32)
        return total + jnp.where(lane == (token & (LANES - 1)), block, 0.0)

    count = ids_ref.shape[1]
    total = lax.fori_loop(0, count, body, jnp.zeros((columns.shape[0], LANES), F32), unroll=8)
    ones = jnp.full((8, LANES), 1.0 / count, F32)
    pooled_ref[...] = lax.dot_general(
        ones,
        total,
        (((1,), (1,)), ((), ())),
        precision=lax.Precision.HIGHEST,
        preferred_element_type=F32,
    )


def pool(prompt_ids, prompt_table, after):
    table_columns = prompt_table.T
    return pl.pallas_call(
        pool_kernel,
        out_shape=jax.ShapeDtypeStruct((8, table_columns.shape[0]), F32),
        in_specs=[smem(), hbm(), anywhere()],
        out_specs=vmem(),
        scratch_shapes=[pltpu.VMEM(table_columns.shape, BF16), pltpu.SemaphoreType.DMA],
        compiler_params=params(),
        cost_estimate=cost(1),
        name="pool_prompt",
    )(prompt_ids, in_hbm(table_columns), after)


def first_kernel(
    places_ref, query_ref, keyval_ref, out_weights_ref, latent_ref, halo_ref, out_cut_ref, *refs
):
    *cut_refs, sems = refs
    head_width = query_ref.shape[1]
    copies = [
        pltpu.make_async_copy(latent_ref.at[: halo_ref.shape[0], :], halo_ref, sems.at[0]),
    ]
    out_rows = out_cut_ref.shape[0]
    at = pl.ds(aligned(places_ref[0] * out_rows, 16), out_rows)
    copies.append(pltpu.make_async_copy(out_weights_ref.at[at, :], out_cut_ref, sems.at[1]))
    for k, target in enumerate(cut_refs):
        rows = target.shape[0]
        at = pl.ds(aligned(places_ref[1 + k] * rows, 16), rows)
        copies += [
            pltpu.make_async_copy(
                query_ref.at[at, :], target.at[:, :head_width], sems.at[2 + 2 * k]
            ),
            pltpu.make_async_copy(
                keyval_ref.at[at, :], target.at[:, head_width:], sems.at[3 + 2 * k]
            ),
        ]
    for copy in copies:
        copy.start()
    for copy in copies:
        copy.wait()


def first_rows(side, places, w_query, w_keyval, w_out, latent):
    quarter = w_query.shape[0] // 4
    columns = w_query.shape[1] + w_keyval.shape[1]
    return pl.pallas_call(
        first_kernel,
        out_shape=[
            jax.ShapeDtypeStruct((SEAM, latent.shape[1]), BF16),
            jax.ShapeDtypeStruct((w_out.shape[0] // 2, w_out.shape[1]), BF16),
        ]
        + [jax.ShapeDtypeStruct((quarter, columns), BF16)] * len(places),
        in_specs=[smem()] + [hbm()] * 4,
        out_specs=[vmem()] * (2 + len(places)),
        scratch_shapes=[pltpu.SemaphoreType.DMA((2 + 2 * len(places),))],
        compiler_params=params(),
        cost_estimate=cost(1),
        name="first_rows",
    )(
        numbers(side, *places),
        *[in_hbm(value) for value in (w_query, w_keyval, w_out, latent)],
    )


def joined(parts):
    return parts[0] if len(parts) == 1 else jnp.concatenate(parts, axis=1)


def can_route(rows):
    return lax.axis_size("var") == 4 and lax.axis_size("tm") % 4 == 0 and rows % 128 == 0


def cut(weights, which, count):
    rows = weights[0].shape[0] // count
    return joined([lax.dynamic_slice_in_dim(w, which * rows, rows, 0) for w in weights])


def gate_kernel(*refs):
    del refs


def together(*values, limit=VMEM_LIMIT):
    return pl.pallas_call(
        gate_kernel,
        out_shape=[jax.ShapeDtypeStruct(v.shape, v.dtype) for v in values],
        in_specs=[anywhere()] * len(values),
        out_specs=[anywhere()] * len(values),
        input_output_aliases={k: k for k in range(len(values))},
        compiler_params=params(limit),
        cost_estimate=cost(1),
        name="gate",
    )(*values)


def numbers(*values):
    return jnp.stack([jnp.asarray(value, jnp.int32) for value in values])


def aligned(value, multiple):
    return pl.multiple_of(value, multiple)


def scale_of(rows_ref, cos_ref, sin_ref):
    rows = rows_ref[...]
    row = jnp.concatenate([rows[k : k + 1, :] for k in range(rows.shape[0])], axis=1)
    return 1.0 + (jnp.concatenate([cos_ref[...], sin_ref[...]], axis=1) + row)


def bias_of(table_ref, last, query_block):
    blocks = table_ref.shape[0]
    biases = []
    for j in range(blocks):
        allowed = table_ref[query_block, j] > 0
        if j == blocks - 1:
            allowed = jnp.logical_and(allowed, last == 0)
        biases.append(jnp.where(allowed, 0.0, MASKED))
    return biases


def normalize(target, begin, ref, scale, width):
    for row in range(0, ref.shape[0], 32):
        values = ref[row : row + 32, :].astype(F32)
        inv_norm = lax.rsqrt(jnp.sum(values * values, axis=-1, keepdims=True) / width + epsilon)
        target[begin + row : begin + row + 32, :] = (values * inv_norm * scale).astype(BF16)


def normalize_kernel(
    latent_ref, halo_ref, rows_ref, cos_ref, sin_ref, normed_ref, window, normed, rows, sems
):
    main_rows = latent_ref.shape[0]
    part = SEAM
    parts = [pl.ds(begin, part) for begin in range(0, window.shape[0], part)]
    sources = [latent_ref.at[at, :] for at in parts[: main_rows // part]] + [halo_ref]
    copies = [pltpu.make_async_copy(rows_ref, rows, sems.at[0])]
    copies += [
        pltpu.make_async_copy(source, window.at[at, :], sems.at[1 + k])
        for k, (source, at) in enumerate(zip(sources, parts))
    ]
    for copy in copies:
        copy.start()
    copies[0].wait()
    scale = scale_of(rows, cos_ref, sin_ref)
    stores = []
    for k, at in enumerate(parts):
        copies[1 + k].wait()
        normalize(normed.at[at, :], 0, window.at[at, :], scale, window.shape[1])
        store = pltpu.make_async_copy(
            normed.at[at, :], normed_ref.at[at, :], sems.at[1 + len(parts) + k]
        )
        store.start()
        stores.append(store)
    for store in stores:
        store.wait()


def normalized(latent, halo, rows, waves):
    shape = (latent.shape[0] + SEAM, latent.shape[1])
    return pl.pallas_call(
        normalize_kernel,
        out_shape=pltpu.HBM(shape, BF16),
        in_specs=[hbm()] * 3 + [vmem()] * 2,
        out_specs=hbm(),
        scratch_shapes=[
            pltpu.VMEM(shape, BF16),
            pltpu.VMEM(shape, BF16),
            pltpu.VMEM(rows.shape, F32),
            pltpu.SemaphoreType.DMA((1 + 2 * (shape[0] // SEAM),)),
        ],
        compiler_params=params(),
        cost_estimate=cost(MICROSECOND),
        name="normalize",
    )(in_hbm(latent), in_hbm(halo), in_hbm(rows), *waves)


def attend_rows(query, keyval_ref, bias, own_block, pair):
    head_width = keyval_ref.shape[1] // 2
    key_rows = keyval_ref.shape[0]
    blocks = len(bias)
    at = pl.ds(pair * LANES, LANES)
    value_at = pl.ds(head_width + pair * LANES, LANES)
    left = lax.broadcasted_iota(jnp.int32, (1, LANES), 1) < HS
    zero = jnp.zeros((), BF16)
    query = query * BF16(1.0 / math.sqrt(HS))
    both = jnp.concatenate([jnp.where(left, query, zero), jnp.where(left, zero, query)], axis=0)
    scores = lax.dot_general(
        both, keyval_ref[:, at], (((1,), (1,)), ((), ())), preferred_element_type=F32
    )
    cut_block = lambda j: scores[:, j * BLK : (j + 1) * BLK]
    peak = None
    for j in range(blocks):
        top = jnp.maximum(cut_block(j), cut_block(blocks + j))
        if j not in (0, own_block):
            top = top + bias[j]
        peak = top if peak is None else jnp.maximum(peak, top)
    peak = jnp.max(peak, axis=-1, keepdims=True)
    offsets = [peak if j in (0, own_block) else peak - bias[j] for j in range(blocks)]
    weights = jnp.concatenate(
        [jnp.exp(cut_block(j) - offsets[j % blocks]).astype(BF16) for j in range(2 * blocks)],
        axis=1,
    )
    ones = jnp.ones((key_rows, LANES), BF16)
    values = jnp.concatenate([keyval_ref[:, value_at], ones], axis=1)
    total = jnp.dot(weights, values, preferred_element_type=F32)
    mixed = total[:, :LANES] / total[:, LANES:]
    return jnp.where(left, mixed[:BLK], mixed[BLK:])


def project_kernel(n_wide, n_pairs, n_sources, places_ref, table_ref, normed_hbm, *refs):
    wide_pieces, refs = refs[:n_wide], refs[n_wide:]
    query_pieces, refs = refs[:n_pairs], refs[n_pairs:]
    keyval_pieces, refs = refs[:n_pairs], refs[n_pairs:]
    sources, refs = refs[:n_sources], refs[n_sources:]
    query_ref, keyval_ref, tail_ref, query_weights, keyval_weights, normed, tail_query, sems = refs
    head_width = query_weights.shape[1]
    window_rows = normed.shape[0] // 2
    main_rows = window_rows - SEAM
    own_rows = pl.ds(0, window_rows)
    source_rows = pl.ds(window_rows, window_rows)
    choice, last = places_ref[0], places_ref[1]

    rows_of = [(places_ref[2 + n_wide + k], p.shape[0]) for k, p in enumerate(query_pieces)]
    rows_of += [(places_ref[2 + k], p.shape[0]) for k, p in enumerate(wide_pieces)]
    rows_of = [pl.ds(aligned(start, 16), count) for start, count in rows_of]
    query_parts = list(query_pieces) + [p.at[:, :head_width] for p in wide_pieces]
    keyval_parts = list(keyval_pieces) + [p.at[:, head_width:] for p in wide_pieces]
    copies = [(normed_hbm, normed.at[own_rows, :])]
    copies += [(p, query_weights.at[at, :]) for p, at in zip(query_parts, rows_of)]
    copies += [(p, keyval_weights.at[at, :]) for p, at in zip(keyval_parts, rows_of)]
    copies = [
        pltpu.make_async_copy(source, target, sems.at[k])
        for k, (source, target) in enumerate(copies)
    ]
    for copy in copies:
        copy.start()
    source_copies = [
        pltpu.make_async_copy(source, normed.at[source_rows, :], sems.at[len(copies)])
        for source in sources
    ]
    for k, copy in enumerate(source_copies):
        pl.when(choice == k)(copy.start)
    for copy in copies[: 1 + len(rows_of)]:
        copy.wait()
    step = 256
    for begin in range(0, head_width, step):
        at = pl.ds(begin, step)
        result = jnp.dot(
            normed[own_rows, :], query_weights[:, at], preferred_element_type=F32
        ).astype(BF16)
        query_ref[:, at] = result[:main_rows]
        tail_query[:, at] = result[main_rows:]
    for k, copy in enumerate(source_copies):
        pl.when(choice == k)(copy.wait)
    for copy in copies[1 + len(rows_of) :]:
        copy.wait()
    for begin in range(0, 2 * head_width, step):
        at = pl.ds(begin, step)
        keyval_ref[:, at] = jnp.dot(
            normed[...], keyval_weights[:, at], preferred_element_type=F32
        ).astype(BF16)
    blocks = window_rows // BLK
    row = lax.broadcasted_iota(jnp.int32, (BLK, 1), 0).astype(F32)
    fade = 1.0 - (row + 0.5) / SEAM
    bias = bias_of(table_ref, last, blocks - 1)
    for pair in range(HEADS // 2):
        at = pl.ds(pair * LANES, LANES)
        mixed = attend_rows(tail_query[:, at], keyval_ref, bias, blocks - 1, pair)
        tail_ref[:, at] = (mixed * fade).astype(BF16)


def project(
    places, block_table, normed, wide, queries, keyvals, sources
):
    window_rows, width = normed.shape
    keyval_width = keyvals[0].shape[1]
    head_width = keyval_width // 2
    n_copies = 1 + 2 * (len(wide) + len(queries))
    arrays = (normed, *wide, *queries, *keyvals, *sources)
    late = (*wide[6:], sources[-1])
    specs = [anywhere() if any(a is b for b in late) else hbm() for a in arrays]
    arrays = [a if any(a is b for b in late) else in_hbm(a) for a in arrays]
    return pl.pallas_call(
        functools.partial(project_kernel, len(wide), len(queries), len(sources)),
        out_shape=[
            jax.ShapeDtypeStruct((window_rows - SEAM, head_width), BF16),
            jax.ShapeDtypeStruct((2 * window_rows, keyval_width), BF16),
            jax.ShapeDtypeStruct((SEAM, head_width), BF16),
        ],
        in_specs=[smem(), smem()] + specs,
        out_specs=[vmem()] * 3,
        scratch_shapes=[
            pltpu.VMEM((width, head_width), BF16),
            pltpu.VMEM((width, keyval_width), BF16),
            pltpu.VMEM((2 * window_rows, width), BF16),
            pltpu.VMEM((SEAM, head_width), BF16),
            pltpu.SemaphoreType.DMA((n_copies + 1,)),
        ],
        compiler_params=params(),
        cost_estimate=cost(10 * MICROSECOND),
        name="project_attend_tail",
    )(
        places,
        block_table,
        *arrays,
    )


def main_kernel(places_ref, table_ref, query_ref, keyval_ref, out_ref):
    blocks = keyval_ref.shape[0] // (2 * BLK)
    for i in range(blocks - 1):
        bias = bias_of(table_ref, places_ref[0], i)
        rows = pl.ds(i * BLK, BLK)
        for pair in range(HEADS // 2):
            at = pl.ds(pair * LANES, LANES)
            out_ref[rows, at] = attend_rows(query_ref[rows, at], keyval_ref, bias, i, pair)


def attend_main(last, block_table, query, keyval):
    rows, width = query.shape
    return pl.pallas_call(
        main_kernel,
        out_shape=jax.ShapeDtypeStruct((rows, width), F32),
        in_specs=[smem(), smem(), vmem(), vmem()],
        out_specs=vmem(),
        compiler_params=params(),
        cost_estimate=cost(4 * MICROSECOND),
        name="attend_main",
    )(numbers(last), block_table, query, keyval)


def finish_kernel(
    n_pieces, places_ref, coef_ref, attended_ref, received_ref, latent_ref, noise_ref, *refs
):
    pieces, (out_ref, weights) = refs[:n_pieces], refs[n_pieces:]
    for k, piece in enumerate(pieces):
        weights[pl.ds(aligned(places_ref[k], 16), piece.shape[0]), :] = piece[...]
    row = lax.broadcasted_iota(jnp.int32, (SEAM, 1), 0).astype(F32)
    ramp_up = jnp.where(coef_ref[3] > 0.5, 1.0, (row + 0.5) / SEAM)
    lead = attended_ref[:SEAM, :] * ramp_up + received_ref[...].astype(F32)
    blended = jnp.concatenate([lead, attended_ref[SEAM:, :]], axis=0).astype(BF16)
    step = 256
    for begin in range(0, out_ref.shape[1], step):
        at = pl.ds(begin, step)
        prediction = jnp.dot(blended, weights[:, at], preferred_element_type=F32)
        result = (
            coef_ref[0] * latent_ref[:, at].astype(F32)
            + coef_ref[1] * prediction
            + coef_ref[2] * noise_ref[:, at].astype(F32)
        )
        out_ref[:, at] = result.astype(BF16)


def finish(coefs, attended, received, latent, noise, pieces, places):
    return pl.pallas_call(
        functools.partial(finish_kernel, len(pieces)),
        out_shape=jax.ShapeDtypeStruct(latent.shape, BF16),
        in_specs=[smem(), smem()] + [vmem()] * (4 + len(pieces)),
        out_specs=vmem(),
        scratch_shapes=[pltpu.VMEM((attended.shape[1], latent.shape[1]), BF16)],
        compiler_params=params(),
        cost_estimate=cost(3 * MICROSECOND),
        name="blend_and_step",
    )(
        places,
        coefs,
        attended,
        received,
        latent,
        noise,
        *pieces,
    )


def from_source(value):
    bits = []
    bit = lax.axis_size("var") // 2
    while bit:
        bits.append(bit)
        bit //= 2
    return [(lax.ppermute(value, "var", [(0, bit)]), bit) for bit in bits]


def passed_on(value, arrivals):
    count = lax.axis_size("var")
    arrays = [value, arrivals[0][0]]
    for array, bit in arrivals[1:]:
        payload = functools.reduce(jnp.add, arrays[1:])
        route = [(i, i + bit) for i in range(2 * bit, count, 2 * bit)]
        arrays.append(array)
        arrays.append(lax.ppermute(payload, "var", route))
    return arrays


def held_by(place):
    bit = lax.axis_size("var") // 2
    choice, count = (place == bit).astype(jnp.int32), 2
    while bit > 1:
        bit //= 2
        choice = jnp.where(place == bit, count, choice)
        choice = jnp.where((place > bit) & (place % (2 * bit) == bit), count + 1, choice)
        count += 2
    return choice


def local(
    latent, fresh_noise, timestep, prompt_ids, block_table, prompt_table, w_query, w_keyval, w_out
):
    latent = latent[0]
    own_rows, model_width = latent.shape
    tm_count = lax.axis_size("tm")
    tm_place = lax.axis_index("tm")
    var_place = lax.axis_index("var")
    rows = w_query.shape[0]
    routed = can_route(rows)
    corner = tm_place & 3

    side = tm_place & 1
    halo_rows, out_cut, *cuts = first_rows(
        side if routed else 0,
        (corner, corner ^ 3) if routed else (),
        w_query,
        w_keyval,
        w_out,
        latent,
    )
    pooled = pool(prompt_ids, prompt_table, halo_rows)
    halo = shifted(halo_rows, "tm", -1)
    current, coef_latent, coef_pred, spread = coefficients(timestep)
    last = tm_place == tm_count - 1
    coefs = jnp.stack([coef_latent, coef_pred, spread, (tm_place == 0).astype(F32)])
    pooled = whole_rows(pooled)
    if routed:
        quarter = rows // 4
        first = swapped(cuts[0], "var", 2)
        fourth = swapped(cuts[1], "var", 2)
        here, there = (var_place ^ 2) * rows, (var_place ^ 3) * rows
        places = [here + (corner ^ k) * quarter for k in range(4)]
        places += [there + (corner ^ k) * quarter for k in (0, 3, 1, 2)]
        places += [var_place * rows, (var_place ^ 1) * rows]
        out_rows = w_out.shape[0]
        half = out_rows // 2
        out_places = [var_place * out_rows, (var_place ^ 1) * out_rows]
        out_places += [(var_place ^ 2) * out_rows + place * half for place in (side, 1 - side)]
        out_places += [(var_place ^ 3) * out_rows + place * half for place in (side, 1 - side)]
        coefs, places, out_places, pooled = together(
            coefs, numbers(held_by(var_place), last, *places), numbers(*out_places), pooled
        )
        halo, pooled, first, fourth = together(
            halo, pooled, first, fourth, limit=ALL_VMEM
        )

    normed = normalized(latent, halo, pooled, time_waves(current, model_width))
    sources = from_source(normed)
    if routed:
        second = swapped(first, "tm", 1)
        third = swapped(first, "tm", 2)
        queries, keyvals = [w_query], [w_keyval]
        fetched = [second, third]
        fetched += [swapped(piece, "var", 1) for piece in (first, fourth, w_query, w_keyval)]
        fetched += [swapped(out_cut, "var", 2)] + [array for array, _ in sources]
        fetched = together(*fetched, limit=ALL_VMEM)
        second, third, first_over, fourth_over, partner_query, partner_keyval, *fetched = fetched
        out_first, *fetched = fetched
        sources = [(array, bit) for array, (_, bit) in zip(fetched, sources)]

        wide = [first, second, third, fourth, first_over, fourth_over]
        wide += [swapped(second, "var", 1), swapped(third, "var", 1)]
        queries, keyvals = [w_query, partner_query], [w_keyval, partner_keyval]
    else:
        wide = []
        queries = [lax.all_gather(w_query, "var", axis=0, tiled=True)]
        keyvals = [lax.all_gather(w_keyval, "var", axis=0, tiled=True)]
        places = numbers(held_by(var_place), last, 0)
        out_places = numbers(0)
    sources = passed_on(normed, sources)
    query, keyval, tail = project(places, block_table, normed, wide, queries, keyvals, sources)
    if routed:
        tail, out_second = together(tail, swapped(out_first, "tm", 1))
        out_pieces = [w_out, swapped(w_out, "var", 1), out_first, out_second]
        out_pieces += [swapped(out_first, "var", 1), swapped(out_second, "var", 1)]
    else:
        out_pieces = [lax.all_gather(w_out, "var", axis=0, tiled=True)]
    received = shifted(tail, "tm", 1)
    attended = attend_main(last, block_table, query, keyval)
    return finish(coefs, attended, received, latent, fresh_noise[0], out_pieces, out_places)[None]


def solution(mesh):
    placed = (
        P("var", "tm", None),
        P("var", "tm", None),
        P(),
        P("var", None),
        P(),
        P(None, "tm"),
        P("var", None),
        P("var", None),
        P("var", None),
    )
    return jax.shard_map(
        local, mesh=mesh, in_specs=placed, out_specs=P("var", "tm", None), check_vma=False
    )
```

```python
import functools
import math

import jax
import jax.numpy as jnp
from jax import lax
from jax.experimental import pallas as pl
from jax.experimental.pallas import tpu as pltpu
from jax.sharding import PartitionSpec as P

HEADS = 12
HS = 64
SEAM = 128
BLK = 128
TSTEPS = 1000
STRIDE = 200
LANES = 128

epsilon = 1e-06
MASKED = -1e30
MICROSECOND = 10**9
VMEM_LIMIT = 18 * 1024 * 1024
ALL_VMEM = 62 * 1024 * 1024

BF16 = jnp.bfloat16
F32 = jnp.float32


def plan(moment):
    return jnp.cos((moment / TSTEPS + 0.008) / 1.008 * (math.pi / 2.0)) ** 2


def coefficients(timestep):
    current = timestep[0].astype(jnp.float32)
    abar_now = plan(current)
    abar_prev = plan(current - STRIDE)
    spread = jnp.sqrt((1.0 - abar_prev) / (1.0 - abar_now) * (1.0 - abar_now / abar_prev))
    carried = jnp.sqrt((1.0 - abar_prev) * (abar_now / abar_prev - abar_now) / (1.0 - abar_now))
    coef_pred = carried - jnp.sqrt(abar_prev) * jnp.sqrt(1.0 - abar_now) / jnp.sqrt(abar_now)
    coef_latent = jnp.sqrt(abar_prev / abar_now)
    return (current, coef_latent, coef_pred, spread)


def time_waves(current, model_width):
    half_width = model_width // 2
    frequency = jnp.exp(-math.log(10000.0) * jnp.arange(half_width, dtype=jnp.float32) / half_width)
    angles = current * frequency
    return (jnp.cos(angles)[None, :], jnp.sin(angles)[None, :])


def swapped(block, axis, bit):
    route = [(i, i ^ bit) for i in range(lax.axis_size(axis))]
    return lax.ppermute(block, axis, route)


def shifted(block, axis, distance):
    devices = range(lax.axis_size(axis))
    route = [(i - distance, i) for i in devices if i - distance in devices]
    return lax.ppermute(block, axis, route)


def vmem():
    return pl.BlockSpec(memory_space=pltpu.VMEM)


def smem():
    return pl.BlockSpec(memory_space=pltpu.SMEM)


def params(limit=VMEM_LIMIT):
    return pltpu.CompilerParams(vmem_limit_bytes=limit)


def anywhere():
    return pl.BlockSpec(memory_space=pl.ANY)


def hbm():
    return pl.BlockSpec(memory_space=pltpu.HBM)


def in_hbm(value):
    return pltpu.with_memory_space_constraint(value, pltpu.HBM)


def cost(flops):
    return pl.CostEstimate(flops=flops, bytes_accessed=1, transcendentals=0)


def whole_rows(row):
    tm_count = lax.axis_size("tm")
    sent = row if row.shape[0] == tm_count else jnp.broadcast_to(row[:1], (tm_count, row.shape[1]))
    arrived = lax.all_to_all(sent, "tm", 0, 0, tiled=True)
    if row.shape[1] % HS or tm_count % 8:
        arrived = arrived.reshape(1, tm_count * row.shape[1])
    return arrived


def pool_kernel(ids_ref, table_ref, after_ref, pooled_ref, columns, sem):
    del after_ref
    whole = pltpu.make_async_copy(table_ref, columns, sem)
    whole.start()
    lane = lax.broadcasted_iota(jnp.int32, (1, LANES), 1)
    whole.wait()

    def body(j, total):
        token = ids_ref[0, j]
        start = pl.multiple_of((token >> 7) * LANES, LANES)
        block = columns[:, pl.ds(start, LANES)].astype(F32)
        return total + jnp.where(lane == (token & (LANES - 1)), block, 0.0)

    count = ids_ref.shape[1]
    total = lax.fori_loop(0, count, body, jnp.zeros((columns.shape[0], LANES), F32), unroll=8)
    ones = jnp.full((8, LANES), 1.0 / count, F32)
    pooled_ref[...] = lax.dot_general(
        ones,
        total,
        (((1,), (1,)), ((), ())),
        precision=lax.Precision.HIGHEST,
        preferred_element_type=F32,
    )


def pool(prompt_ids, prompt_table, after):
    table_columns = prompt_table.T
    return pl.pallas_call(
        pool_kernel,
        out_shape=jax.ShapeDtypeStruct((8, table_columns.shape[0]), F32),
        in_specs=[smem(), hbm(), anywhere()],
        out_specs=vmem(),
        scratch_shapes=[pltpu.VMEM(table_columns.shape, BF16), pltpu.SemaphoreType.DMA],
        compiler_params=params(),
        cost_estimate=cost(1),
        name="pool_prompt",
    )(prompt_ids, in_hbm(table_columns), after)


def first_kernel(
    places_ref, query_ref, keyval_ref, out_weights_ref, latent_ref, halo_ref, out_cut_ref, *refs
):
    *cut_refs, sems = refs
    head_width = query_ref.shape[1]
    copies = [
        pltpu.make_async_copy(latent_ref.at[: halo_ref.shape[0], :], halo_ref, sems.at[0]),
    ]
    out_rows = out_cut_ref.shape[0]
    at = pl.ds(aligned(places_ref[0] * out_rows, 16), out_rows)
    copies.append(pltpu.make_async_copy(out_weights_ref.at[at, :], out_cut_ref, sems.at[1]))
    for k, target in enumerate(cut_refs):
        rows = target.shape[0]
        at = pl.ds(aligned(places_ref[1 + k] * rows, 16), rows)
        copies += [
            pltpu.make_async_copy(
                query_ref.at[at, :], target.at[:, :head_width], sems.at[2 + 2 * k]
            ),
            pltpu.make_async_copy(
                keyval_ref.at[at, :], target.at[:, head_width:], sems.at[3 + 2 * k]
            ),
        ]
    for copy in copies:
        copy.start()
    for copy in copies:
        copy.wait()


def first_rows(side, places, w_query, w_keyval, w_out, latent):
    quarter = w_query.shape[0] // 4
    columns = w_query.shape[1] + w_keyval.shape[1]
    return pl.pallas_call(
        first_kernel,
        out_shape=[
            jax.ShapeDtypeStruct((SEAM, latent.shape[1]), BF16),
            jax.ShapeDtypeStruct((w_out.shape[0] // 2, w_out.shape[1]), BF16),
        ]
        + [jax.ShapeDtypeStruct((quarter, columns), BF16)] * len(places),
        in_specs=[smem()] + [hbm()] * 4,
        out_specs=[vmem()] * (2 + len(places)),
        scratch_shapes=[pltpu.SemaphoreType.DMA((2 + 2 * len(places),))],
        compiler_params=params(),
        cost_estimate=cost(1),
        name="first_rows",
    )(
        numbers(side, *places),
        *[in_hbm(value) for value in (w_query, w_keyval, w_out, latent)],
    )


def joined(parts):
    return parts[0] if len(parts) == 1 else jnp.concatenate(parts, axis=1)


def can_route(rows):
    return lax.axis_size("var") == 4 and lax.axis_size("tm") % 4 == 0 and rows % 128 == 0


def cut(weights, which, count):
    rows = weights[0].shape[0] // count
    return joined([lax.dynamic_slice_in_dim(w, which * rows, rows, 0) for w in weights])


def gate_kernel(*refs):
    del refs


def together(*values, limit=VMEM_LIMIT):
    return pl.pallas_call(
        gate_kernel,
        out_shape=[jax.ShapeDtypeStruct(v.shape, v.dtype) for v in values],
        in_specs=[anywhere()] * len(values),
        out_specs=[anywhere()] * len(values),
        input_output_aliases={k: k for k in range(len(values))},
        compiler_params=params(limit),
        cost_estimate=cost(1),
        name="gate",
    )(*values)


def numbers(*values):
    return jnp.stack([jnp.asarray(value, jnp.int32) for value in values])


def aligned(value, multiple):
    return pl.multiple_of(value, multiple)


def scale_of(rows_ref, cos_ref, sin_ref):
    rows = rows_ref[...]
    row = jnp.concatenate([rows[k : k + 1, :] for k in range(rows.shape[0])], axis=1)
    return 1.0 + (jnp.concatenate([cos_ref[...], sin_ref[...]], axis=1) + row)


def bias_of(table_ref, last, query_block):
    blocks = table_ref.shape[0]
    biases = []
    for j in range(blocks):
        allowed = table_ref[query_block, j] > 0
        if j == blocks - 1:
            allowed = jnp.logical_and(allowed, last == 0)
        biases.append(jnp.where(allowed, 0.0, MASKED))
    return biases


def normalize(target, begin, ref, scale, width):
    for row in range(0, ref.shape[0], 32):
        values = ref[row : row + 32, :].astype(F32)
        inv_norm = lax.rsqrt(jnp.sum(values * values, axis=-1, keepdims=True) / width + epsilon)
        target[begin + row : begin + row + 32, :] = (values * inv_norm * scale).astype(BF16)


def normalize_kernel(
    latent_ref, halo_ref, rows_ref, cos_ref, sin_ref, normed_ref, window, normed, rows, sems
):
    main_rows = latent_ref.shape[0]
    part = SEAM
    parts = [pl.ds(begin, part) for begin in range(0, window.shape[0], part)]
    sources = [latent_ref.at[at, :] for at in parts[: main_rows // part]] + [halo_ref]
    copies = [pltpu.make_async_copy(rows_ref, rows, sems.at[0])]
    copies += [
        pltpu.make_async_copy(source, window.at[at, :], sems.at[1 + k])
        for k, (source, at) in enumerate(zip(sources, parts))
    ]
    for copy in copies:
        copy.start()
    copies[0].wait()
    scale = scale_of(rows, cos_ref, sin_ref)
    stores = []
    for k, at in enumerate(parts):
        copies[1 + k].wait()
        normalize(normed.at[at, :], 0, window.at[at, :], scale, window.shape[1])
        store = pltpu.make_async_copy(
            normed.at[at, :], normed_ref.at[at, :], sems.at[1 + len(parts) + k]
        )
        store.start()
        stores.append(store)
    for store in stores:
        store.wait()


def normalized(latent, halo, rows, waves):
    shape = (latent.shape[0] + SEAM, latent.shape[1])
    return pl.pallas_call(
        normalize_kernel,
        out_shape=pltpu.HBM(shape, BF16),
        in_specs=[hbm()] * 3 + [vmem()] * 2,
        out_specs=hbm(),
        scratch_shapes=[
            pltpu.VMEM(shape, BF16),
            pltpu.VMEM(shape, BF16),
            pltpu.VMEM(rows.shape, F32),
            pltpu.SemaphoreType.DMA((1 + 2 * (shape[0] // SEAM),)),
        ],
        compiler_params=params(),
        cost_estimate=cost(MICROSECOND),
        name="normalize",
    )(in_hbm(latent), in_hbm(halo), in_hbm(rows), *waves)


def attend_rows(query, keyval_ref, bias, own_block, pair):
    head_width = keyval_ref.shape[1] // 2
    key_rows = keyval_ref.shape[0]
    blocks = len(bias)
    at = pl.ds(pair * LANES, LANES)
    value_at = pl.ds(head_width + pair * LANES, LANES)
    left = lax.broadcasted_iota(jnp.int32, (1, LANES), 1) < HS
    zero = jnp.zeros((), BF16)
    query = query * BF16(1.0 / math.sqrt(HS))
    both = jnp.concatenate([jnp.where(left, query, zero), jnp.where(left, zero, query)], axis=0)
    scores = lax.dot_general(
        both, keyval_ref[:, at], (((1,), (1,)), ((), ())), preferred_element_type=F32
    )
    cut_block = lambda j: scores[:, j * BLK : (j + 1) * BLK]
    peak = None
    for j in range(blocks):
        top = jnp.maximum(cut_block(j), cut_block(blocks + j))
        if j not in (0, own_block):
            top = top + bias[j]
        peak = top if peak is None else jnp.maximum(peak, top)
    peak = jnp.max(peak, axis=-1, keepdims=True)
    offsets = [peak if j in (0, own_block) else peak - bias[j] for j in range(blocks)]
    weights = jnp.concatenate(
        [jnp.exp(cut_block(j) - offsets[j % blocks]).astype(BF16) for j in range(2 * blocks)],
        axis=1,
    )
    ones = jnp.ones((key_rows, LANES), BF16)
    values = jnp.concatenate([keyval_ref[:, value_at], ones], axis=1)
    total = jnp.dot(weights, values, preferred_element_type=F32)
    mixed = total[:, :LANES] / total[:, LANES:]
    return jnp.where(left, mixed[:BLK], mixed[BLK:])


def project_kernel(n_wide, n_pairs, n_sources, places_ref, table_ref, normed_hbm, *refs):
    wide_pieces, refs = refs[:n_wide], refs[n_wide:]
    query_pieces, refs = refs[:n_pairs], refs[n_pairs:]
    keyval_pieces, refs = refs[:n_pairs], refs[n_pairs:]
    sources, refs = refs[:n_sources], refs[n_sources:]
    query_ref, keyval_ref, tail_ref, query_weights, keyval_weights, normed, tail_query, sems = refs
    head_width = query_weights.shape[1]
    window_rows = normed.shape[0] // 2
    main_rows = window_rows - SEAM
    own_rows = pl.ds(0, window_rows)
    source_rows = pl.ds(window_rows, window_rows)
    choice, last = places_ref[0], places_ref[1]

    rows_of = [(places_ref[2 + n_wide + k], p.shape[0]) for k, p in enumerate(query_pieces)]
    rows_of += [(places_ref[2 + k], p.shape[0]) for k, p in enumerate(wide_pieces)]
    rows_of = [pl.ds(aligned(start, 16), count) for start, count in rows_of]
    query_parts = list(query_pieces) + [p.at[:, :head_width] for p in wide_pieces]
    keyval_parts = list(keyval_pieces) + [p.at[:, head_width:] for p in wide_pieces]
    copies = [(normed_hbm, normed.at[own_rows, :])]
    copies += [(p, query_weights.at[at, :]) for p, at in zip(query_parts, rows_of)]
    copies += [(p, keyval_weights.at[at, :]) for p, at in zip(keyval_parts, rows_of)]
    copies = [
        pltpu.make_async_copy(source, target, sems.at[k])
        for k, (source, target) in enumerate(copies)
    ]
    for copy in copies:
        copy.start()
    source_copies = [
        pltpu.make_async_copy(source, normed.at[source_rows, :], sems.at[len(copies)])
        for source in sources
    ]
    for k, copy in enumerate(source_copies):
        pl.when(choice == k)(copy.start)
    for copy in copies[: 1 + len(rows_of)]:
        copy.wait()
    step = 256
    for begin in range(0, head_width, step):
        at = pl.ds(begin, step)
        result = jnp.dot(
            normed[own_rows, :], query_weights[:, at], preferred_element_type=F32
        ).astype(BF16)
        query_ref[:, at] = result[:main_rows]
        tail_query[:, at] = result[main_rows:]
    for k, copy in enumerate(source_copies):
        pl.when(choice == k)(copy.wait)
    for copy in copies[1 + len(rows_of) :]:
        copy.wait()
    for begin in range(0, 2 * head_width, step):
        at = pl.ds(begin, step)
        keyval_ref[:, at] = jnp.dot(
            normed[...], keyval_weights[:, at], preferred_element_type=F32
        ).astype(BF16)
    blocks = window_rows // BLK
    row = lax.broadcasted_iota(jnp.int32, (BLK, 1), 0).astype(F32)
    fade = 1.0 - (row + 0.5) / SEAM
    bias = bias_of(table_ref, last, blocks - 1)
    for pair in range(HEADS // 2):
        at = pl.ds(pair * LANES, LANES)
        mixed = attend_rows(tail_query[:, at], keyval_ref, bias, blocks - 1, pair)
        tail_ref[:, at] = (mixed * fade).astype(BF16)


def project(
    places, block_table, normed, wide, queries, keyvals, sources
):
    window_rows, width = normed.shape
    keyval_width = keyvals[0].shape[1]
    head_width = keyval_width // 2
    n_copies = 1 + 2 * (len(wide) + len(queries))
    arrays = (normed, *wide, *queries, *keyvals, *sources)
    late = (*wide[6:], sources[-1], queries[0], keyvals[0])
    specs = [anywhere() if any(a is b for b in late) else hbm() for a in arrays]
    arrays = [a if any(a is b for b in late) else in_hbm(a) for a in arrays]
    return pl.pallas_call(
        functools.partial(project_kernel, len(wide), len(queries), len(sources)),
        out_shape=[
            jax.ShapeDtypeStruct((window_rows - SEAM, head_width), BF16),
            jax.ShapeDtypeStruct((2 * window_rows, keyval_width), BF16),
            jax.ShapeDtypeStruct((SEAM, head_width), BF16),
        ],
        in_specs=[smem(), smem()] + specs,
        out_specs=[vmem()] * 3,
        scratch_shapes=[
            pltpu.VMEM((width, head_width), BF16),
            pltpu.VMEM((width, keyval_width), BF16),
            pltpu.VMEM((2 * window_rows, width), BF16),
            pltpu.VMEM((SEAM, head_width), BF16),
            pltpu.SemaphoreType.DMA((n_copies + 1,)),
        ],
        compiler_params=params(),
        cost_estimate=cost(10 * MICROSECOND),
        name="project_attend_tail",
    )(
        places,
        block_table,
        *arrays,
    )


def main_kernel(places_ref, table_ref, query_ref, keyval_ref, out_ref):
    blocks = keyval_ref.shape[0] // (2 * BLK)
    for i in range(blocks - 1):
        bias = bias_of(table_ref, places_ref[0], i)
        rows = pl.ds(i * BLK, BLK)
        for pair in range(HEADS // 2):
            at = pl.ds(pair * LANES, LANES)
            out_ref[rows, at] = attend_rows(query_ref[rows, at], keyval_ref, bias, i, pair)


def attend_main(last, block_table, query, keyval):
    rows, width = query.shape
    return pl.pallas_call(
        main_kernel,
        out_shape=jax.ShapeDtypeStruct((rows, width), F32),
        in_specs=[smem(), smem(), vmem(), vmem()],
        out_specs=vmem(),
        compiler_params=params(),
        cost_estimate=cost(4 * MICROSECOND),
        name="attend_main",
    )(numbers(last), block_table, query, keyval)


def finish_kernel(
    n_pieces, places_ref, coef_ref, attended_ref, received_ref, latent_ref, noise_ref, *refs
):
    pieces, (out_ref, weights) = refs[:n_pieces], refs[n_pieces:]
    for k, piece in enumerate(pieces):
        weights[pl.ds(aligned(places_ref[k], 16), piece.shape[0]), :] = piece[...]
    row = lax.broadcasted_iota(jnp.int32, (SEAM, 1), 0).astype(F32)
    ramp_up = jnp.where(coef_ref[3] > 0.5, 1.0, (row + 0.5) / SEAM)
    lead = attended_ref[:SEAM, :] * ramp_up + received_ref[...].astype(F32)
    blended = jnp.concatenate([lead, attended_ref[SEAM:, :]], axis=0).astype(BF16)
    step = 256
    for begin in range(0, out_ref.shape[1], step):
        at = pl.ds(begin, step)
        prediction = jnp.dot(blended, weights[:, at], preferred_element_type=F32)
        result = (
            coef_ref[0] * latent_ref[:, at].astype(F32)
            + coef_ref[1] * prediction
            + coef_ref[2] * noise_ref[:, at].astype(F32)
        )
        out_ref[:, at] = result.astype(BF16)


def finish(coefs, attended, received, latent, noise, pieces, places):
    return pl.pallas_call(
        functools.partial(finish_kernel, len(pieces)),
        out_shape=jax.ShapeDtypeStruct(latent.shape, BF16),
        in_specs=[smem(), smem()] + [vmem()] * (4 + len(pieces)),
        out_specs=vmem(),
        scratch_shapes=[pltpu.VMEM((attended.shape[1], latent.shape[1]), BF16)],
        compiler_params=params(),
        cost_estimate=cost(3 * MICROSECOND),
        name="blend_and_step",
    )(
        places,
        coefs,
        attended,
        received,
        latent,
        noise,
        *pieces,
    )


def from_source(value):
    bits = []
    bit = lax.axis_size("var") // 2
    while bit:
        bits.append(bit)
        bit //= 2
    return [(lax.ppermute(value, "var", [(0, bit)]), bit) for bit in bits]


def passed_on(value, arrivals):
    count = lax.axis_size("var")
    arrays = [value, arrivals[0][0]]
    for array, bit in arrivals[1:]:
        payload = functools.reduce(jnp.add, arrays[1:])
        route = [(i, i + bit) for i in range(2 * bit, count, 2 * bit)]
        arrays.append(array)
        arrays.append(lax.ppermute(payload, "var", route))
    return arrays


def held_by(place):
    bit = lax.axis_size("var") // 2
    choice, count = (place == bit).astype(jnp.int32), 2
    while bit > 1:
        bit //= 2
        choice = jnp.where(place == bit, count, choice)
        choice = jnp.where((place > bit) & (place % (2 * bit) == bit), count + 1, choice)
        count += 2
    return choice


def local(
    latent, fresh_noise, timestep, prompt_ids, block_table, prompt_table, w_query, w_keyval, w_out
):
    latent = latent[0]
    own_rows, model_width = latent.shape
    tm_count = lax.axis_size("tm")
    tm_place = lax.axis_index("tm")
    var_place = lax.axis_index("var")
    rows = w_query.shape[0]
    routed = can_route(rows)
    corner = tm_place & 3

    side = tm_place & 1
    halo_rows, out_cut, *cuts = first_rows(
        side if routed else 0,
        (corner, corner ^ 3) if routed else (),
        w_query,
        w_keyval,
        w_out,
        latent,
    )
    pooled = pool(prompt_ids, prompt_table, halo_rows)
    halo = shifted(halo_rows, "tm", -1)
    current, coef_latent, coef_pred, spread = coefficients(timestep)
    last = tm_place == tm_count - 1
    coefs = jnp.stack([coef_latent, coef_pred, spread, (tm_place == 0).astype(F32)])
    pooled = whole_rows(pooled)
    if routed:
        quarter = rows // 4
        first = swapped(cuts[0], "var", 2)
        fourth = swapped(cuts[1], "var", 2)
        here, there = (var_place ^ 2) * rows, (var_place ^ 3) * rows
        places = [here + (corner ^ k) * quarter for k in range(4)]
        places += [there + (corner ^ k) * quarter for k in (0, 3, 1, 2)]
        places += [var_place * rows, (var_place ^ 1) * rows]
        out_rows = w_out.shape[0]
        half = out_rows // 2
        out_places = [var_place * out_rows, (var_place ^ 1) * out_rows]
        out_places += [(var_place ^ 2) * out_rows + place * half for place in (side, 1 - side)]
        out_places += [(var_place ^ 3) * out_rows + place * half for place in (side, 1 - side)]
        coefs, places, out_places, pooled = together(
            coefs, numbers(held_by(var_place), last, *places), numbers(*out_places), pooled
        )
        halo, pooled, first, fourth = together(
            halo, pooled, first, fourth, limit=ALL_VMEM
        )

    normed = normalized(latent, halo, pooled, time_waves(current, model_width))
    sources = from_source(normed)
    if routed:
        second = swapped(first, "tm", 1)
        third = swapped(first, "tm", 2)
        queries, keyvals = [w_query], [w_keyval]
        fetched = [second, third]
        fetched += [swapped(piece, "var", 1) for piece in (first, fourth, w_query, w_keyval)]
        fetched += [swapped(out_cut, "var", 2)] + [array for array, _ in sources]
        fetched = together(*fetched, limit=ALL_VMEM)
        second, third, first_over, fourth_over, partner_query, partner_keyval, *fetched = fetched
        out_first, *fetched = fetched
        sources = [(array, bit) for array, (_, bit) in zip(fetched, sources)]

        wide = [first, second, third, fourth, first_over, fourth_over]
        wide += [swapped(second, "var", 1), swapped(third, "var", 1)]
        queries, keyvals = [w_query, partner_query], [w_keyval, partner_keyval]
    else:
        wide = []
        queries = [lax.all_gather(w_query, "var", axis=0, tiled=True)]
        keyvals = [lax.all_gather(w_keyval, "var", axis=0, tiled=True)]
        places = numbers(held_by(var_place), last, 0)
        out_places = numbers(0)
    sources = passed_on(normed, sources)
    query, keyval, tail = project(places, block_table, normed, wide, queries, keyvals, sources)
    if routed:
        tail, out_second = together(tail, swapped(out_first, "tm", 1))
        out_pieces = [w_out, swapped(w_out, "var", 1), out_first, out_second]
        out_pieces += [swapped(out_first, "var", 1), swapped(out_second, "var", 1)]
    else:
        out_pieces = [lax.all_gather(w_out, "var", axis=0, tiled=True)]
    received = shifted(tail, "tm", 1)
    attended = attend_main(last, block_table, query, keyval)
    return finish(coefs, attended, received, latent, fresh_noise[0], out_pieces, out_places)[None]


def solution(mesh):
    placed = (
        P("var", "tm", None),
        P("var", "tm", None),
        P(),
        P("var", None),
        P(),
        P(None, "tm"),
        P("var", None),
        P("var", None),
        P("var", None),
    )
    return jax.shard_map(
        local, mesh=mesh, in_specs=placed, out_specs=P("var", "tm", None), check_vma=False
    )
```
